128 devices in a mesh: dp: 32 (over x, y, core), mp: 2 (over z_lo), tower: 2 (over z_hi).
Axes of the slice: x: 4, y: 4, z: 4 (z_hi: 2, z_lo: 2; z = z_hi * 2 + z_lo), core: 2. Of those that a mesh axis runs over, the one named last changes fastest.
Arguments:
- features: bfloat16 [2, 16384, 1536], P('tower', 'dp'), may hold values from -16 to 16
- projection: bfloat16 [2, 1536, 1536], P('tower', None, 'mp'), may hold values from -1 to 1
- similarity_scale: float32 [1], replicated, may hold values from 8 to 16
- logit_bias: float32 [1], replicated, may hold values from -6 to -2
Outputs:
- row_loss: float32 [2, 16384], P('tower', ('dp', 'mp'))
- projection_grad: float32 [2, 1536, 1536], P('tower', None, 'mp')
The draws below stay inside these ranges and needn't reach their ends.
All inputs are finite; a program needn't handle non-finite values.
Results may differ from the reference program's by a relative error of at most 0.00049.
Values may be sent and summed in bfloat16 or wider, within the bound.
No kernel may reach another device: no remote copies, remote signals or barrier semaphores. Data moves between devices by JAX's collectives and lax.ppermute only.
A program may use at most 192 MiB of HBM per device.

```python
import math
import jax
import jax.numpy as jnp
from jax import lax

E = 1536
ROWS_DEV = 512
BATCH = 16384


def draw_features(key, part):
    key = jax.random.fold_in(key, 7)
    keys = jax.random.split(key, 6)
    centers = jax.random.truncated_normal(keys[0], -3.0, 3.0, (16, E), jnp.float32)
    member = jax.random.randint(keys[1], (BATCH,), 0, 16)
    strength = jax.random.uniform(keys[2], (BATCH, 1), jnp.float32, 0.0, 1.5)
    paired = jax.random.uniform(keys[3], (BATCH, 1), jnp.float32, 0.75, 0.97)
    own_noise = jax.random.truncated_normal(keys[4], -3.0, 3.0, (BATCH, E), jnp.float32)
    text_noise = jax.random.truncated_normal(keys[5], -3.0, 3.0, (BATCH, E), jnp.float32)
    chosen = jnp.take(centers, member, axis=0)
    image = (strength * chosen + own_noise) / jnp.sqrt(1.0 + strength * strength)
    text = paired * image + jnp.sqrt(1.0 - paired * paired) * text_noise
    stacked = jnp.stack([image, text])
    return jnp.clip(stacked, -16.0, 16.0).astype(jnp.bfloat16)


def draw_projection(key, part):
    key = jax.random.fold_in(key, 19)
    first_key, second_key = jax.random.split(key, 2)
    base = jax.random.truncated_normal(first_key, -3.0, 3.0, (E, E), jnp.float32)
    other = jax.random.truncated_normal(second_key, -3.0, 3.0, (E, E), jnp.float32)
    factor = 1.0 / math.sqrt(E)
    head_image = base * factor
    head_text = (0.9 * base + 0.436 * other) * factor
    return jnp.stack([head_image, head_text]).astype(jnp.bfloat16)


def setup_inputs(seed: int = 0) -> dict:
    seeds = jax.random.split(jax.random.key(seed), 5)
    features = draw_features(jax.random.fold_in(seeds[4], 71), 0)
    projection = draw_projection(jax.random.fold_in(seeds[4], 71), 0)
    similarity_scale = jnp.clip(jax.random.uniform(seeds[2], (1,), jnp.float32, 8.0, 16.0), 8.0, 16.0)
    logit_bias = jnp.clip(jax.random.uniform(seeds[3], (1,), jnp.float32, -6.0, -2.0), -6.0, -2.0)
    return {"features": features, "projection": projection, "similarity_scale": similarity_scale, "logit_bias": logit_bias}


def project_side(inputs, weight):
    projected = jnp.dot(inputs, weight, preferred_element_type=jnp.float32)
    inverse = lax.rsqrt(lax.optimization_barrier(jnp.sum(projected * projected, axis=1, keepdims=True)) + 1e-06)
    return (projected, inverse, (projected * inverse).astype(jnp.bfloat16))

def proj_grad_side(projected, inverse, grad_embed):
    along = lax.optimization_barrier(jnp.sum(projected * grad_embed, axis=1, keepdims=True))
    cubed = inverse * inverse * inverse
    return (inverse * grad_embed - cubed * projected * along).astype(jnp.bfloat16)

def reference(features, projection, similarity_scale, logit_bias):
    batch_rows = features.shape[1]
    width = features.shape[2]
    batch_as_float = jnp.float32(batch_rows)
    scale_factor = similarity_scale[0]
    row_offset = logit_bias[0]
    image_proj, image_inv, image_embed = project_side(features[0], projection[0])
    text_proj, text_inv, text_vectors = project_side(features[1], projection[1])
    text_ids = jnp.arange(batch_rows, dtype=jnp.int32)

    def step_block(running_sums, block_number):
        first_row = (block_number * ROWS_DEV).astype(jnp.int32)
        image_row_block = lax.dynamic_slice_in_dim(image_embed, first_row, ROWS_DEV, 0)
        image_ids = first_row + jnp.arange(ROWS_DEV, dtype=jnp.int32)
        pair_logits = scale_factor * lax.dot_general(image_row_block, text_vectors, (((1,), (1,)), ((), ())), preferred_element_type=jnp.float32) + row_offset
        labels = jnp.where(image_ids[:, None] == text_ids[None, :], 1.0, -1.0).astype(pair_logits.dtype)
        losses = jax.nn.softplus(-labels * pair_logits)
        pair_coefficient = (-labels * jax.nn.sigmoid(-labels * pair_logits) / batch_as_float).astype(jnp.bfloat16)
        image_loss = lax.optimization_barrier(jnp.sum(losses, axis=1)) / batch_as_float
        image_gradient = scale_factor * jnp.dot(pair_coefficient, text_vectors, preferred_element_type=jnp.float32)
        text_loss = running_sums[0] + lax.optimization_barrier(jnp.sum(losses, axis=0)) / batch_as_float
        text_gradient = running_sums[1] + scale_factor * lax.dot_general(pair_coefficient, image_row_block, (((0,), (0,)), ((), ())), preferred_element_type=jnp.float32)
        return ((text_loss, text_gradient), (image_loss, image_gradient))
    start_totals = (jnp.zeros((batch_rows,), jnp.float32), jnp.zeros((batch_rows, width), jnp.float32))
    block_numbers = jnp.arange(batch_rows // ROWS_DEV, dtype=jnp.int32)
    (text_loss, text_gradient), (image_loss, image_gradient) = lax.scan(step_block, start_totals, block_numbers)
    image_loss = image_loss.reshape(batch_rows)
    image_gradient = image_gradient.reshape(batch_rows, width)
    image_gp = proj_grad_side(image_proj, image_inv, image_gradient)
    text_gp = proj_grad_side(text_proj, text_inv, text_gradient)
    image_weight = lax.dot_general(features[0], image_gp, (((0,), (0,)), ((), ())), preferred_element_type=jnp.float32)
    text_weight = lax.dot_general(features[1], text_gp, (((0,), (0,)), ((), ())), preferred_element_type=jnp.float32)
    return (jnp.stack([image_loss, text_loss]), jnp.stack([image_weight, text_weight]))
```

```python
import functools

import jax
import jax.numpy as jnp
from jax import lax
from jax.experimental import pallas as pl
from jax.experimental.pallas import tpu as pltpu
from jax.sharding import Mesh, PartitionSpec as P

F32 = jnp.float32
BF16 = jnp.bfloat16
Z = ("m", "t")


def shifted(value, axes, step):
    count = lax.axis_size(axes)
    number = (lambda i: i % 2 * 2 + i // 2) if axes == Z else (lambda i: i)
    route = [(number(i), number((i + step) % count)) for i in range(count)]
    return lax.ppermute(value, axes, route)


def pick(block, index, size, axis=0):
    return lax.dynamic_slice_in_dim(block, index * size, size, axis)


def from_sources(own, send, axes, place):
    return [own] + [shifted(send((place + k) % 4), axes, k) for k in (2, 1, 3)]


ORDER = (0, 2, 1, 3)


def by_source(pieces, place):
    stacked = jnp.zeros((4,) + pieces[0].shape, pieces[0].dtype)
    for k, piece in zip(ORDER, pieces):
        stacked = lax.dynamic_update_index_in_dim(stacked, piece, (place - k) % 4, 0)
    return stacked


def tile_kernel(
    diag_ref, scale_ref, a_ref, b_ref, ga_ref, gb_ref, la_ref, lb_ref, acc_ref, loss_ref, c_ref
):
    step = pl.program_id(0)
    rows, width = a_ref.shape
    cols = b_ref.shape[0]
    sub = 256
    scale = scale_ref[0]
    bias = scale_ref[1]
    texts = b_ref[...]

    @pl.when(step == 0)
    def _():
        acc_ref[...] = jnp.zeros_like(acc_ref)
        loss_ref[...] = jnp.zeros_like(loss_ref)

    column_loss = jnp.zeros((1, cols), F32)
    for part in range(rows // sub):
        here = pl.ds(part * sub, sub)
        logits = (
            lax.dot_general(
                a_ref[here, :], texts, (((1,), (1,)), ((), ())), preferred_element_type=F32
            )
            * scale
            + bias
        )
        image = lax.broadcasted_iota(jnp.int32, (sub, cols), 0) + part * sub
        text = lax.broadcasted_iota(jnp.int32, (sub, cols), 1) + step * cols
        same = (text - image) == diag_ref[0]
        same = jnp.logical_and(same, (image // sub) == diag_ref[1])
        grown = jnp.exp(jnp.where(same, -logits, logits))
        whole = 1.0 + grown
        inverse = 1.0 / whole
        losses = jnp.log(whole) + (grown - (whole - 1.0)) * inverse
        share = grown * inverse
        c_ref[here, :] = jnp.where(same, -share, share).astype(BF16)
        loss_ref[here, :] += sum(
            losses[:, k * 128 : (k + 1) * 128] for k in range(cols // 128)
        )
        column_loss += jnp.sum(losses, axis=0, keepdims=True)
    lb_ref[0] = column_loss
    coefficient = c_ref[...]
    acc_ref[...] += jnp.dot(coefficient, texts, preferred_element_type=F32)
    gb_ref[...] = lax.dot_general(
        coefficient, a_ref[...], (((0,), (0,)), ((), ())), preferred_element_type=F32
    ).astype(gb_ref.dtype)

    @pl.when(step == pl.num_programs(0) - 1)
    def _():
        ga_ref[...] = acc_ref[...].astype(ga_ref.dtype)
        la_ref[...] = jnp.sum(loss_ref[...], axis=1, keepdims=True)


def tile_terms(images, texts, diag, scales):
    rows, width = images.shape
    count = texts.shape[0]
    cols = 512
    steps = count // cols
    smem = pl.BlockSpec(memory_space=pltpu.SMEM)
    return pl.pallas_call(
        tile_kernel,
        grid=(steps,),
        in_specs=[
            smem,
            smem,
            pl.BlockSpec((rows, width), lambda j: (0, 0)),
            pl.BlockSpec((cols, width), lambda j: (j, 0)),
        ],
        out_specs=[
            pl.BlockSpec((rows, width), lambda j: (0, 0)),
            pl.BlockSpec((cols, width), lambda j: (j, 0)),
            pl.BlockSpec((rows, 1), lambda j: (0, 0)),
            pl.BlockSpec((1, 1, cols), lambda j: (j, 0, 0)),
        ],
        out_shape=[
            jax.ShapeDtypeStruct((rows, width), BF16),
            jax.ShapeDtypeStruct((count, width), BF16),
            jax.ShapeDtypeStruct((rows, 1), F32),
            jax.ShapeDtypeStruct((steps, 1, cols), F32),
        ],
        scratch_shapes=[
            pltpu.VMEM((rows, width), F32),
            pltpu.VMEM((rows, 128), F32),
            pltpu.VMEM((rows, cols), BF16),
        ],
        compiler_params=pltpu.CompilerParams(vmem_limit_bytes=56 * 2**20),
        cost_estimate=pl.CostEstimate(
            flops=6 * rows * count * width,
            bytes_accessed=4 * (rows + count) * width,
            transcendentals=3 * rows * count,
        ),
    )(diag, scales, images, texts)


def summed_piece(blocks, axis, place):
    pieces = from_sources(
        lax.dynamic_index_in_dim(blocks, place, 0, False),
        lambda d: lax.dynamic_index_in_dim(blocks, d, 0, False),
        axis,
        place,
    )
    return sum(piece.astype(F32) for piece in pieces)


def gathered(block, axis, place):
    return by_source(from_sources(block, lambda d: block, axis, place), place)


def on_device(features, projection, similarity_scale, logit_bias):
    x, y, c = lax.axis_index("x"), lax.axis_index("y"), lax.axis_index("c")
    m, t = lax.axis_index("m"), lax.axis_index("t")
    z = t * 2 + m
    inputs = features[0]
    rows, width = inputs.shape
    weight = projection[0]
    half = weight.shape[1]
    part = rows // 2
    pairs = rows * 32
    scale_factor = similarity_scale[0]

    projected = jnp.dot(inputs, weight, preferred_element_type=F32)
    squares = lax.psum(jnp.sum(projected * projected, axis=1), "m")[:, None]
    inverse = lax.rsqrt(squares + 1e-06)
    embedded = (projected * inverse).astype(BF16)
    mine = pick(inputs, c, half, 1)
    others = shifted(pick(inputs, 1 - c, half, 1), "c", 1)

    def rows_for(d):
        return pick(embedded, jnp.where(t == 0, d % 2, d // 2), part)

    arrived = by_source(from_sources(rows_for(z), rows_for, Z, z), z)
    image = jnp.concatenate([arrived[0], arrived[1]], axis=1)
    text = jnp.concatenate([arrived[2], arrived[3]], axis=1)

    images = gathered(image, "y", y).reshape(4 * part, width)
    texts_core = gathered(text, "x", x)
    texts_other = shifted(texts_core, "c", 1)
    first = jnp.where(c == 0, texts_core, texts_other)
    second = jnp.where(c == 0, texts_other, texts_core)
    texts = jnp.stack([first, second]).reshape(8 * part, width)

    offset = ((c * 4 + x) - y) * part
    diag = jnp.stack([offset, jnp.where(m == t, y, -1)]).astype(jnp.int32)
    scales = jnp.stack([scale_factor, logit_bias[0]])
    grad_a, grad_b, loss_a, loss_b = tile_terms(images, texts, diag, scales)

    grad_a = summed_piece(grad_a.reshape(4, part, width), "y", y)
    grad_b = grad_b.reshape(2, 4, part, width)
    kept = lax.dynamic_index_in_dim(grad_b, c, 0, False)
    given = shifted(lax.dynamic_index_in_dim(grad_b, 1 - c, 0, False), "c", 1)
    grad_b = summed_piece((kept.astype(F32) + given.astype(F32)).astype(BF16), "x", x)

    both = jnp.stack([grad_a, grad_b]).astype(BF16)

    def columns_for(d):
        return pick(lax.dynamic_index_in_dim(both, d // 2, 0, False), d % 2, half, 1)

    arrived = by_source(from_sources(columns_for(z), columns_for, Z, z), z).astype(F32)
    from_image = jnp.stack([arrived[0] + arrived[2], arrived[1] + arrived[3]])
    from_text = jnp.stack([arrived[0] + arrived[1], arrived[2] + arrived[3]])
    grad_embed = jnp.where(t == 0, from_image, from_text).reshape(rows, half)
    grad_embed = grad_embed * (scale_factor / pairs)

    along = lax.psum(jnp.sum(projected * grad_embed, axis=1), "m")[:, None]
    cubed = inverse * inverse * inverse
    grad_proj = (inverse * grad_embed - cubed * projected * along).astype(BF16)
    grad_other = shifted(grad_proj, "c", 1)
    weight_part = lax.dot_general(
        mine, grad_proj, (((0,), (0,)), ((), ())), preferred_element_type=F32
    ) + lax.dot_general(others, grad_other, (((0,), (0,)), ((), ())), preferred_element_type=F32)

    quarter = half // 2
    one = summed_piece(weight_part[:quarter].reshape(4, quarter // 4, half), "x", x)
    two = summed_piece(weight_part[quarter:].reshape(4, quarter // 4, half), "y", y)
    one = sum(from_sources(one, lambda d: one, "y", y))
    two = sum(from_sources(two, lambda d: two, "x", x))
    one = gathered(one, "x", x).reshape(quarter, half)
    two = gathered(two, "y", y).reshape(quarter, half)
    whole = jnp.concatenate([one, two], axis=0)
    swapped = shifted(whole, "c", 1)
    weight_grad = jnp.concatenate(
        [jnp.where(c == 0, whole, swapped), jnp.where(c == 0, swapped, whole)], axis=0
    )

    loss_a = summed_piece(loss_a.reshape(4, part), "y", y)
    loss_a = loss_a + shifted(loss_a, "t", 1)
    loss_b = loss_b.reshape(2, 4, part)
    loss_b = lax.dynamic_index_in_dim(loss_b, c, 0, False) + shifted(
        lax.dynamic_index_in_dim(loss_b, 1 - c, 0, False), "c", 1
    )
    loss_b = summed_piece(loss_b, "x", x)
    loss_b = loss_b + shifted(loss_b, "m", 1)
    loss_b = jnp.where(t == m, loss_b, shifted(loss_b, "t", 1))
    row_loss = jnp.where(t == 0, loss_a, loss_b) / pairs
    return (row_loss[None], weight_grad[None])


def solution(mesh):
    fine = Mesh(mesh.devices.reshape(4, 4, 2, 2, 2), ("x", "y", "c", "m", "t"))
    dp = ("x", "y", "c")
    placed = (P("t", dp, None), P("t", None, "m"), P(), P())
    return jax.shard_map(
        on_device,
        mesh=fine,
        in_specs=placed,
        out_specs=(P("t", dp + ("m",)), P("t", None, "m")),
        check_vma=False,
    )
```

```python
import jax
import jax.numpy as jnp
from jax import lax
from jax.experimental import pallas as pl
from jax.experimental.pallas import tpu as pltpu
from jax.sharding import Mesh, PartitionSpec as P

F32 = jnp.float32
BF16 = jnp.bfloat16
STEPS = (2, 1, 3)


def shifted(value, axis, step):
    count = lax.axis_size(axis)
    return lax.ppermute(value, axis, [(i, (i + step) % count) for i in range(count)])


def crossed(value, tower, half):
    flip = 2 * half + tower
    return lax.ppermute(value, ("m", "t"), [(i, i ^ flip) for i in range(4)])


def pick(block, index, size, axis=0):
    return lax.dynamic_slice_in_dim(block, index * size, size, axis)


def tied(*values):
    return lax.optimization_barrier(values)


def tile_kernel(diag_ref, scale_ref, *refs):
    rows_refs, cols_refs = refs[:4], refs[4:12]
    ga_refs, gb_refs, la_ref, lb_ref = refs[12:16], refs[16:24], refs[24], refs[25]
    acc_ref, loss_ref = refs[26], refs[27]
    part, width = rows_refs[0].shape
    scale = scale_ref[0]
    bias = scale_ref[1]
    for step in range(4):
        gb = [jnp.zeros((part, width), F32) for _ in range(2)]
        for r in range(4):
            here = pl.ds(r * part, part)
            images = rows_refs[r][...]
            grad = jnp.zeros((part, width), F32)
            for core in range(2):
                texts = cols_refs[2 * step + core][...]
                logits = (
                    lax.dot_general(
                        images, texts, (((1,), (1,)), ((), ())), preferred_element_type=F32
                    )
                    * scale
                    + bias
                )
                if step == 0 and r == 0 and core == 0:
                    image = lax.broadcasted_iota(jnp.int32, (part, part), 0)
                    text = lax.broadcasted_iota(jnp.int32, (part, part), 1)
                    same = image + diag_ref[0] == text
                    logits = jnp.where(same, -logits, logits)
                grown = jnp.exp(logits)
                whole = 1.0 + grown
                inverse = 1.0 / whole
                losses = jnp.log(whole) + (grown - (whole - 1.0)) * inverse
                share = grown * inverse
                if step == 0 and r == 0 and core == 0:
                    share = jnp.where(same, -share, share)
                coefficient = share.astype(BF16)
                folded = sum(losses[:, k * 128 : (k + 1) * 128] for k in range(part // 128))
                column = jnp.sum(losses, axis=0, keepdims=True)
                if step == 0 and core == 0:
                    loss_ref[here, :] = folded
                else:
                    loss_ref[here, :] += folded
                if r == 0:
                    lb_ref[2 * step + core] = column
                else:
                    lb_ref[2 * step + core] += column
                grad += jnp.dot(coefficient, texts, preferred_element_type=F32)
                gb[core] += lax.dot_general(
                    coefficient, images, (((0,), (0,)), ((), ())), preferred_element_type=F32
                )
            if step == 0:
                acc_ref[here, :] = grad
            elif step < 3:
                acc_ref[here, :] += grad
            else:
                ga_refs[r][...] = (acc_ref[here, :] + grad).astype(BF16)
        for core in range(2):
            gb_refs[2 * step + core][...] = gb[core].astype(BF16)
    la_ref[...] = jnp.sum(loss_ref[...], axis=1, keepdims=True)


def tile_terms(rows, cols, diag, scales):
    part, width = rows[0].shape
    smem = pl.BlockSpec(memory_space=pltpu.SMEM)
    vmem = pl.BlockSpec(memory_space=pltpu.VMEM)
    piece = jax.ShapeDtypeStruct((part, width), BF16)
    out = pl.pallas_call(
        tile_kernel,
        in_specs=[smem, smem] + [vmem] * 12,
        out_specs=[vmem] * 14,
        out_shape=[piece] * 12
        + [
            jax.ShapeDtypeStruct((4 * part, 1), F32),
            jax.ShapeDtypeStruct((8, 1, part), F32),
        ],
        scratch_shapes=[
            pltpu.VMEM((4 * part, width), F32),
            pltpu.VMEM((4 * part, 128), F32),
        ],
        compiler_params=pltpu.CompilerParams(vmem_limit_bytes=56 * 2**20),
        cost_estimate=pl.CostEstimate(
            flops=6 * 4 * 8 * part * part * width,
            bytes_accessed=2 * 24 * part * width,
            transcendentals=3 * 32 * part * part,
        ),
    )(diag, scales, *rows, *cols)
    return out[:4], out[4:12], out[12], out[13]


def on_device(features, projection, similarity_scale, logit_bias):
    x, y, c = lax.axis_index("x"), lax.axis_index("y"), lax.axis_index("c")
    m, t = lax.axis_index("m"), lax.axis_index("t")
    inputs = features[0]
    rows, width = inputs.shape
    weight = projection[0]
    half = weight.shape[1]
    part = rows // 2
    pairs = rows * 32
    scale_factor = similarity_scale[0]

    projected = jnp.dot(inputs, weight, preferred_element_type=F32)
    squares = lax.psum(jnp.sum(projected * projected, axis=1), "m")[:, None]
    inverse = lax.rsqrt(squares + 1e-06)
    embedded = (projected * inverse).astype(BF16)
    mine = pick(inputs, c, half, 1)
    others = shifted(pick(inputs, 1 - c, half, 1), "c", 1)

    def rows_for(tower, flip):
        return pick(embedded, jnp.where(t == 0, m ^ flip, 1 ^ tower), part)

    kept = rows_for(0, 0)
    far, near, cross = tied(
        crossed(rows_for(1, 0), 1, 0), crossed(rows_for(0, 1), 0, 1), crossed(rows_for(1, 1), 1, 1)
    )
    own = jnp.concatenate([kept, near], axis=1)
    other = jnp.concatenate([far, cross], axis=1)
    own, other = tied(own, other)

    r2, c2, r1, c1, r3, c3 = tied(
        *(shifted(v, a, k) for k in STEPS for v, a in ((own, "y"), (other, "x")))
    )
    row_pieces = [own, r1, r2, r3]
    col_pieces = [other, c1, c2, c3]
    col_others = [shifted(piece, "c", 1) for piece in col_pieces]
    diag = jnp.where(m == t, 0, 2 * part).astype(jnp.int32).reshape(1)
    scales = jnp.stack([scale_factor, logit_bias[0]])
    cols = [piece for both in zip(col_pieces, col_others) for piece in both]
    grad_rows, grad_cols, loss_rows, loss_cols = tile_terms(row_pieces, cols, diag, scales)

    given = [shifted(grad_cols[2 * k + 1], "c", 1) for k in range(4)]
    sums = [(grad_cols[2 * k].astype(F32) + given[k].astype(F32)).astype(BF16) for k in range(4)]
    r2, c2, r1, c1, r3, c3 = tied(
        *(shifted(v[k], a, 4 - k) for k in STEPS for v, a in ((grad_rows, "y"), (sums, "x")))
    )
    grad_own = sum(v.astype(F32) for v in (grad_rows[0], r1, r2, r3)).astype(BF16)
    grad_other = sum(v.astype(F32) for v in (sums[0], c1, c2, c3)).astype(BF16)

    loss_rows = loss_rows.reshape(4, part)
    loss_rows = loss_rows[0] + sum(shifted(loss_rows[k], "y", 4 - k) for k in STEPS)
    loss_cols = loss_cols.reshape(4, 2, part)
    loss_cols = loss_cols[:, 0] + shifted(loss_cols[:, 1], "c", 1)
    loss_cols = loss_cols[0] + sum(shifted(loss_cols[k], "x", 4 - k) for k in STEPS)
    loss_far = crossed(loss_cols, 1, 0)
    loss_near = crossed(jnp.where(m == 0, loss_rows, loss_far), 0, 1)
    kept = jnp.where(jnp.logical_and(t == 1, m == 0), 0.0, loss_rows)
    row_loss = (kept + jnp.where(jnp.logical_and(t == 1, m == 1), 0.0, loss_far)) + jnp.where(
        t == 1, loss_near, 0.0
    )
    row_loss = row_loss / pairs

    far, near, cross = tied(
        crossed(grad_other[:, :half], 1, 0),
        crossed(grad_own[:, half:], 0, 1),
        crossed(grad_other[:, half:], 1, 1),
    )
    g00, g10, g01, g11 = (v.astype(F32) for v in (grad_own[:, :half], far, near, cross))
    first = jnp.where(t == 0, jnp.where(m == 0, g00 + g10, g01 + g11), g10 + g11)
    second = jnp.where(t == 0, jnp.where(m == 0, g01 + g11, g00 + g10), g00 + g01)
    grad_embed = jnp.concatenate([first, second], axis=0) * (scale_factor / pairs)
    grad_embed, row_loss = tied(grad_embed, row_loss)

    along = lax.psum(jnp.sum(projected * grad_embed, axis=1), "m")[:, None]
    cubed = inverse * inverse * inverse
    grad_proj = (inverse * grad_embed - cubed * projected * along).astype(BF16)
    grad_swap = shifted(grad_proj, "c", 1)
    weight_part = lax.dot_general(
        mine, grad_proj, (((0,), (0,)), ((), ())), preferred_element_type=F32
    ) + lax.dot_general(others, grad_swap, (((0,), (0,)), ((), ())), preferred_element_type=F32)

    quarter = half // 2
    small = quarter // 4
    one, two = weight_part[:quarter], weight_part[quarter:]
    a2, b2, a1, b1, a3, b3 = tied(
        *(
            shifted(pick(v, (p + k) % 4, small), a, k)
            for k in STEPS
            for v, p, a in ((one, x, "x"), (two, y, "y"))
        )
    )
    one = pick(one, x, small) + a1 + a2 + a3
    two = pick(two, y, small) + b1 + b2 + b3
    a2, b2, a1, b1, a3, b3 = tied(
        *(shifted(v, a, k) for k in STEPS for v, a in ((one, "y"), (two, "x")))
    )
    one = one + a1 + a2 + a3
    two = two + b1 + b2 + b3
    a2, b2, a1, b1, a3, b3 = tied(
        *(shifted(v, a, k) for k in STEPS for v, a in ((one, "x"), (two, "y")))
    )
    whole = jnp.zeros((half, half), F32)
    for k, (a, b) in enumerate(((one, two), (a1, b1), (a2, b2), (a3, b3))):
        whole = lax.dynamic_update_slice_in_dim(whole, a, (x - k) % 4 * small, 0)
        whole = lax.dynamic_update_slice_in_dim(whole, b, quarter + (y - k) % 4 * small, 0)
    swapped = shifted(whole, "c", 1)
    weight_grad = jnp.zeros((2, half, half), F32)
    weight_grad = lax.dynamic_update_index_in_dim(weight_grad, whole, c, 0)
    weight_grad = lax.dynamic_update_index_in_dim(weight_grad, swapped, 1 - c, 0)
    return (row_loss[None], weight_grad.reshape(1, width, half))


def solution(mesh):
    fine = Mesh(mesh.devices.reshape(4, 4, 2, 2, 2), ("x", "y", "c", "m", "t"))
    dp = ("x", "y", "c")
    placed = (P("t", dp, None), P("t", None, "m"), P(), P())
    return jax.shard_map(
        on_device,
        mesh=fine,
        in_specs=placed,
        out_specs=(P("t", dp + ("m",)), P("t", None, "m")),
        check_vma=False,
    )
```

```python
import jax
import jax.numpy as jnp
from jax import lax
from jax.experimental import pallas as pl
from jax.experimental.pallas import tpu as pltpu
from jax.sharding import Mesh, PartitionSpec as P

F32 = jnp.float32
BF16 = jnp.bfloat16
STEPS = (2, 1, 3)


def shifted(value, axis, step):
    count = lax.axis_size(axis)
    return lax.ppermute(value, axis, [(i, (i + step) % count) for i in range(count)])


def crossed(value, tower, half):
    flip = 2 * half + tower
    return lax.ppermute(value, ("m", "t"), [(i, i ^ flip) for i in range(4)])


def pick(block, index, size, axis=0):
    return lax.dynamic_slice_in_dim(block, index * size, size, axis)


def tied(*values):
    return lax.optimization_barrier(values)


def tile_kernel(diag_ref, scale_ref, *refs):
    rows_refs, cols_refs = refs[:4], refs[4:12]
    ga_refs, gb_refs, la_ref, lb_ref = refs[12:16], refs[16:24], refs[24], refs[25]
    acc_ref, loss_ref = refs[26], refs[27]
    part, width = rows_refs[0].shape
    scale = scale_ref[0]
    bias = scale_ref[1]
    for step in range(4):
        gb = [jnp.zeros((part, width), F32) for _ in range(2)]
        for r in range(4):
            here = pl.ds(r * part, part)
            images = rows_refs[r][...]
            grad = jnp.zeros((part, width), F32)
            for core in range(2):
                texts = cols_refs[2 * step + core][...]
                logits = (
                    lax.dot_general(
                        images, texts, (((1,), (1,)), ((), ())), preferred_element_type=F32
                    )
                    * scale
                    + bias
                )
                if step == 0 and r == 0 and core == 0:
                    image = lax.broadcasted_iota(jnp.int32, (part, part), 0)
                    text = lax.broadcasted_iota(jnp.int32, (part, part), 1)
                    same = image + diag_ref[0] == text
                    logits = jnp.where(same, -logits, logits)
                grown = jnp.exp(logits)
                whole = 1.0 + grown
                inverse = 1.0 / whole
                losses = jnp.log(whole) + (grown - (whole - 1.0)) * inverse
                share = grown * inverse
                if step == 0 and r == 0 and core == 0:
                    share = jnp.where(same, -share, share)
                coefficient = share.astype(BF16)
                folded = sum(losses[:, k * 128 : (k + 1) * 128] for k in range(part // 128))
                column = jnp.sum(losses, axis=0, keepdims=True)
                if step == 0 and core == 0:
                    loss_ref[here, :] = folded
                else:
                    loss_ref[here, :] += folded
                if r == 0:
                    lb_ref[2 * step + core] = column
                else:
                    lb_ref[2 * step + core] += column
                grad += jnp.dot(coefficient, texts, preferred_element_type=F32)
                gb[core] += lax.dot_general(
                    coefficient, images, (((0,), (0,)), ((), ())), preferred_element_type=F32
                )
            if step == 0:
                acc_ref[here, :] = grad
            elif step < 3:
                acc_ref[here, :] += grad
            else:
                ga_refs[r][...] = (acc_ref[here, :] + grad).astype(BF16)
        for core in range(2):
            gb_refs[2 * step + core][...] = gb[core].astype(BF16)
    la_ref[...] = jnp.sum(loss_ref[...], axis=1, keepdims=True)


def tile_terms(rows, cols, diag, scales):
    part, width = rows[0].shape
    smem = pl.BlockSpec(memory_space=pltpu.SMEM)
    vmem = pl.BlockSpec(memory_space=pltpu.VMEM)
    piece = jax.ShapeDtypeStruct((part, width), BF16)
    out = pl.pallas_call(
        tile_kernel,
        in_specs=[smem, smem] + [vmem] * 12,
        out_specs=[vmem] * 14,
        out_shape=[piece] * 12
        + [
            jax.ShapeDtypeStruct((4 * part, 1), F32),
            jax.ShapeDtypeStruct((8, 1, part), F32),
        ],
        scratch_shapes=[
            pltpu.VMEM((4 * part, width), F32),
            pltpu.VMEM((4 * part, 128), F32),
        ],
        compiler_params=pltpu.CompilerParams(vmem_limit_bytes=56 * 2**20),
        cost_estimate=pl.CostEstimate(
            flops=6 * 4 * 8 * part * part * width,
            bytes_accessed=2 * 24 * part * width,
            transcendentals=3 * 32 * part * part,
        ),
    )(diag, scales, *rows, *cols)
    return out[:4], out[4:12], out[12], out[13]


def on_device(features, projection, similarity_scale, logit_bias):
    x, y, c = lax.axis_index("x"), lax.axis_index("y"), lax.axis_index("c")
    m, t = lax.axis_index("m"), lax.axis_index("t")
    inputs = features[0]
    rows, width = inputs.shape
    weight = projection[0]
    half = weight.shape[1]
    part = rows // 2
    pairs = rows * 32
    scale_factor = similarity_scale[0]

    projected = jnp.dot(inputs, weight, preferred_element_type=F32)
    squares = lax.psum(jnp.sum(projected * projected, axis=1), "m")[:, None]
    inverse = lax.rsqrt(squares + 1e-06)
    embedded = (projected * inverse).astype(BF16)
    mine = pick(inputs, c, half, 1)
    others = shifted(pick(inputs, 1 - c, half, 1), "c", 1)

    def rows_for(tower, flip):
        return pick(embedded, jnp.where(t == 0, m ^ flip, 1 ^ tower), part)

    kept = rows_for(0, 0)
    far, near, cross = tied(
        crossed(rows_for(1, 0), 1, 0), crossed(rows_for(0, 1), 0, 1), crossed(rows_for(1, 1), 1, 1)
    )
    own = jnp.concatenate([kept, near], axis=1)
    other = jnp.concatenate([far, cross], axis=1)
    own, other = tied(own, other)

    cut = part // 2
    r1, r3, c1, c3, d0 = tied(
        shifted(own, "y", 1),
        shifted(own, "y", 3),
        shifted(other, "x", 1),
        shifted(other, "x", 3),
        shifted(other, "c", 1),
    )
    c2a, c2b, r2a, r2b = tied(
        shifted(c1[:cut], "x", 1),
        shifted(c3[cut:], "x", 3),
        shifted(r1[:cut], "y", 1),
        shifted(r3[cut:], "y", 3),
    )
    d1, d3 = shifted(c1, "c", 1), shifted(c3, "c", 1)
    c2 = jnp.concatenate([c2a, c2b], axis=0)
    d2 = shifted(c2, "c", 1)
    r2 = jnp.concatenate([r2a, r2b], axis=0)
    diag = jnp.where(m == t, 0, 2 * part).astype(jnp.int32).reshape(1)
    scales = jnp.stack([scale_factor, logit_bias[0]])
    grad_rows, grad_cols, loss_rows, loss_cols = tile_terms(
        [own, r1, r2, r3], [other, d0, c1, d1, c2, d2, c3, d3], diag, scales
    )

    def joined(k):
        given = shifted(grad_cols[2 * k + 1], "c", 1)
        return (grad_cols[2 * k].astype(F32) + given.astype(F32)).astype(BF16)

    s2, s1, s3, s0 = joined(2), joined(1), joined(3), joined(0)
    g0, g1, g2, g3 = grad_rows
    f1, f3, e1, e3 = tied(
        shifted(g2[:cut], "y", 1),
        shifted(g2[cut:], "y", 3),
        shifted(s2[:cut], "x", 1),
        shifted(s2[cut:], "x", 3),
    )

    def added(block, top, bottom):
        parts = [block[:cut].astype(F32), block[cut:].astype(F32)]
        if top is not None:
            parts[0] += top.astype(F32)
        if bottom is not None:
            parts[1] += bottom.astype(F32)
        return jnp.concatenate(parts, axis=0).astype(BF16)

    f3, f1, e3, e1 = tied(
        shifted(added(g3, f1, None), "y", 1),
        shifted(added(g1, None, f3), "y", 3),
        shifted(added(s3, e1, None), "x", 1),
        shifted(added(s1, None, e3), "x", 3),
    )
    grad_own = g0.astype(F32) + f1.astype(F32) + f3.astype(F32)
    grad_other = s0.astype(F32) + e1.astype(F32) + e3.astype(F32)

    loss_rows = loss_rows.reshape(4, part)
    loss_rows = loss_rows[0] + sum(shifted(loss_rows[k], "y", 4 - k) for k in STEPS)
    loss_cols = loss_cols.reshape(4, 2, part)
    loss_cols = loss_cols[:, 0] + shifted(loss_cols[:, 1], "c", 1)
    loss_cols = loss_cols[0] + sum(shifted(loss_cols[k], "x", 4 - k) for k in STEPS)
    line_own = jnp.stack([jnp.sum(own.astype(F32) * grad_own, axis=1), loss_rows])
    line_other = jnp.stack([jnp.sum(other.astype(F32) * grad_other, axis=1), loss_cols])
    grad_own, grad_other = grad_own.astype(BF16), grad_other.astype(BF16)

    h10, h01, h11, far, near, cross = tied(
        crossed(line_other, 1, 0),
        crossed(line_own, 0, 1),
        crossed(line_other, 1, 1),
        crossed(grad_other[:, :half], 1, 0),
        crossed(grad_own[:, half:], 0, 1),
        crossed(grad_other[:, half:], 1, 1),
    )

    def halves(v00, v10, v01, v11):
        first = jnp.where(t == 0, jnp.where(m == 0, v00 + v10, v01 + v11), v10 + v11)
        second = jnp.where(t == 0, jnp.where(m == 0, v01 + v11, v00 + v10), v00 + v01)
        return first, second

    first, second = halves(*(v.astype(F32) for v in (grad_own[:, :half], far, near, cross)))
    grad_embed = jnp.concatenate([first, second], axis=0) * (scale_factor / pairs)
    first, second = halves(line_own, h10, h01, h11)
    along = jnp.concatenate([first[0], second[0]])[:, None] * (scale_factor / pairs)
    row_loss = jnp.where(m == 0, first[1], second[1]) / pairs

    grad_proj = (inverse * grad_embed - inverse * inverse * projected * along).astype(BF16)
    grad_swap = shifted(grad_proj, "c", 1)
    weight_part = lax.dot_general(
        mine, grad_proj, (((0,), (0,)), ((), ())), preferred_element_type=F32
    ) + lax.dot_general(others, grad_swap, (((0,), (0,)), ((), ())), preferred_element_type=F32)

    small = half // 4
    lead = jnp.where(c == 0, x, y)
    back = jnp.where(c == 0, y, x)
    a2, a1, a3 = tied(
        *(turned(pick(weight_part, (lead + k) % 4, small), 0, k) for k in STEPS)
    )
    piece = pick(weight_part, lead, small) + a1 + a2 + a3
    a2, a1, a3 = tied(*(turned(piece, 1, k) for k in STEPS))
    piece = (piece + a2) + (a1 + a3)
    pieces = [piece] + [turned(piece, 0, k) for k in (1, 3, 2)]
    swapped = [shifted(v, "c", 1) for v in pieces]
    places = [c * half + (lead - k) % 4 * small for k in (0, 1, 3, 2)]
    places += [(1 - c) * half + (back - k) % 4 * small for k in (0, 1, 3, 2)]
    weight_grad = placed_rows(jnp.stack(places).astype(jnp.int32), pieces + swapped)
    return (row_loss[None], weight_grad[None])


def turned(value, late, step):
    route = []
    for i in range(32):
        x, y, c = i // 8, i // 2 % 4, i % 2
        if c ^ late:
            y = (y + step) % 4
        else:
            x = (x + step) % 4
        route.append((i, x * 8 + y * 2 + c))
    return lax.ppermute(value, ("x", "y", "c"), route)


def place_kernel(places_ref, *refs):
    out_ref = refs[-1]
    for i, ref in enumerate(refs[:-1]):
        size = ref.shape[0]
        out_ref[pl.ds(pl.multiple_of(places_ref[i], size), size), :] = ref[...]


def placed_rows(places, pieces):
    size, width = pieces[0].shape
    vmem = pl.BlockSpec(memory_space=pltpu.VMEM)
    return pl.pallas_call(
        place_kernel,
        in_specs=[pl.BlockSpec(memory_space=pltpu.SMEM)] + [vmem] * len(pieces),
        out_specs=vmem,
        out_shape=jax.ShapeDtypeStruct((size * len(pieces), width), F32),
        compiler_params=pltpu.CompilerParams(vmem_limit_bytes=32 * 2**20),
    )(places, *pieces)


def solution(mesh):
    fine = Mesh(mesh.devices.reshape(4, 4, 2, 2, 2), ("x", "y", "c", "m", "t"))
    dp = ("x", "y", "c")
    placed = (P("t", dp, None), P("t", None, "m"), P(), P())
    return jax.shard_map(
        on_device,
        mesh=fine,
        in_specs=placed,
        out_specs=(P("t", dp + ("m",)), P("t", None, "m")),
        check_vma=False,
    )
```

```python
import jax
import jax.numpy as jnp
from jax import lax
from jax.experimental import pallas as pl
from jax.experimental.pallas import tpu as pltpu
from jax.sharding import Mesh, PartitionSpec as P

F32 = jnp.float32
BF16 = jnp.bfloat16
STEPS = (2, 1, 3)
EXTRA = 16


def shifted(value, axis, step):
    count = lax.axis_size(axis)
    return lax.ppermute(value, axis, [(i, (i + step) % count) for i in range(count)])


def crossed(value, tower, half):
    flip = 2 * half + tower
    return lax.ppermute(value, ("m", "t"), [(i, i ^ flip) for i in range(4)])


def pick(block, index, size, axis=0):
    return lax.dynamic_slice_in_dim(block, index * size, size, axis)


def tied(*values):
    return lax.optimization_barrier(values)


def tile_kernel(diag_ref, scale_ref, *refs):
    rows_refs, cols_refs = refs[:5], refs[5:15]
    ga_refs, gb_refs, la_ref, lb_ref = refs[15:19], refs[19:27], refs[27], refs[28]
    acc_ref, loss_ref = refs[29], refs[30]
    part, width = rows_refs[0].shape

    def block(refs, k):
        if k < 3:
            return refs[k][...]
        return jnp.concatenate([refs[3][...], refs[4][...]], axis=0)

    scale = scale_ref[0]
    bias = scale_ref[1]
    for step in range(4):
        gb = [jnp.zeros((part, width), F32) for _ in range(2)]
        for r in range(4):
            here = pl.ds(r * part, part)
            images = block(rows_refs, r)
            grad = jnp.zeros((part, width), F32)
            for core in range(2):
                texts = block(cols_refs[5 * core : 5 * core + 5], step)
                logits = (
                    lax.dot_general(
                        images, texts, (((1,), (1,)), ((), ())), preferred_element_type=F32
                    )
                    * scale
                    + bias
                )
                if step == 0 and r == 0 and core == 0:
                    image = lax.broadcasted_iota(jnp.int32, (part, part), 0)
                    text = lax.broadcasted_iota(jnp.int32, (part, part), 1)
                    same = image + diag_ref[0] == text
                    logits = jnp.where(same, -logits, logits)
                grown = jnp.exp(logits)
                whole = 1.0 + grown
                inverse = 1.0 / whole
                losses = jnp.log(whole) + (grown - (whole - 1.0)) * inverse
                share = grown * inverse
                if step == 0 and r == 0 and core == 0:
                    share = jnp.where(same, -share, share)
                coefficient = share.astype(BF16)
                folded = sum(losses[:, k * 128 : (k + 1) * 128] for k in range(part // 128))
                column = jnp.sum(losses, axis=0, keepdims=True)
                if step == 0 and core == 0:
                    loss_ref[here, :] = folded
                else:
                    loss_ref[here, :] += folded
                if r == 0:
                    lb_ref[4 * core + step] = column
                else:
                    lb_ref[4 * core + step] += column
                grad += jnp.dot(coefficient, texts, preferred_element_type=F32)
                gb[core] += lax.dot_general(
                    coefficient, images, (((0,), (0,)), ((), ())), preferred_element_type=F32
                )
            if step == 0:
                acc_ref[here, :] = grad
            elif step < 3:
                acc_ref[here, :] += grad
            else:
                ga_refs[r][...] = (acc_ref[here, :] + grad).astype(BF16)
        for core in range(2):
            gb_refs[4 * core + step][...] = gb[core].astype(BF16)
    for r in range(4):
        la_ref[r] = jnp.sum(loss_ref[pl.ds(r * part, part), :].T, axis=0, keepdims=True)


def tile_terms(rows, cols, diag, scales):
    part, width = rows[0].shape
    smem = pl.BlockSpec(memory_space=pltpu.SMEM)
    vmem = pl.BlockSpec(memory_space=pltpu.VMEM)
    piece = jax.ShapeDtypeStruct((part, width), BF16)
    out = pl.pallas_call(
        tile_kernel,
        in_specs=[smem, smem] + [vmem] * 15,
        out_specs=[vmem] * 14,
        out_shape=[piece] * 12
        + [
            jax.ShapeDtypeStruct((4, 1, part), F32),
            jax.ShapeDtypeStruct((8, 1, part), F32),
        ],
        scratch_shapes=[
            pltpu.VMEM((4 * part, width), F32),
            pltpu.VMEM((4 * part, 128), F32),
        ],
        compiler_params=pltpu.CompilerParams(vmem_limit_bytes=56 * 2**20),
        cost_estimate=pl.CostEstimate(
            flops=6 * 4 * 8 * part * part * width,
            bytes_accessed=2 * 24 * part * width,
            transcendentals=3 * 32 * part * part,
        ),
    )(diag, scales, *rows, *cols)
    return out[:4], out[4:12], out[12], out[13]


def on_device(features, projection, similarity_scale, logit_bias):
    x, y, c = lax.axis_index("x"), lax.axis_index("y"), lax.axis_index("c")
    m, t = lax.axis_index("m"), lax.axis_index("t")
    inputs = features[0]
    rows, width = inputs.shape
    weight = projection[0]
    half = weight.shape[1]
    part = rows // 2
    pairs = rows * 32
    scale_factor = similarity_scale[0]

    projected = jnp.dot(inputs, weight, preferred_element_type=F32)
    squares = lax.psum(jnp.sum(projected * projected, axis=1), "m")[:, None]
    inverse = lax.rsqrt(squares + 1e-06)
    embedded = (projected * inverse).astype(BF16)
    mine = pick(inputs, c, half, 1)
    others = shifted(pick(inputs, 1 - c, half, 1), "c", 1)

    def rows_for(tower, flip):
        return pick(embedded, jnp.where(t == 0, m ^ flip, 1 ^ tower), part)

    kept = rows_for(0, 0)
    far, near, cross = tied(
        crossed(rows_for(1, 0), 1, 0), crossed(rows_for(0, 1), 0, 1), crossed(rows_for(1, 1), 1, 1)
    )
    own = jnp.concatenate([kept, near], axis=1)
    other = jnp.concatenate([far, cross], axis=1)
    own, other = tied(own, other)

    cut = part // 2
    r1, r3, c1, c3, d0 = tied(
        shifted(own, "y", 1),
        shifted(own, "y", 3),
        shifted(other, "x", 1),
        shifted(other, "x", 3),
        shifted(other, "c", 1),
    )
    c2a, c2b, r2a, r2b = tied(
        shifted(c1[:cut], "x", 1),
        shifted(c3[cut:], "x", 3),
        shifted(r1[:cut], "y", 1),
        shifted(r3[cut:], "y", 3),
    )
    d1, d3 = shifted(c1, "c", 1), shifted(c3, "c", 1)
    d2a, d2b = shifted(c2a, "c", 1), shifted(c2b, "c", 1)
    diag = jnp.where(m == t, 0, 2 * part).astype(jnp.int32).reshape(1)
    scales = jnp.stack([scale_factor, logit_bias[0]])
    grad_rows, grad_cols, loss_rows, loss_cols = tile_terms(
        [own, r1, r3, r2a, r2b], [other, c1, c3, c2a, c2b, d0, d1, d3, d2a, d2b], diag, scales
    )
    g0, g1, g3, g2 = grad_rows

    def joined(k):
        given = shifted(grad_cols[4 + k], "c", 1)
        return (grad_cols[k].astype(F32) + given.astype(F32)).astype(BF16)

    s2 = joined(3)
    f1, f3, e1, e3 = tied(
        shifted(g2[:cut], "y", 1),
        shifted(g2[cut:], "y", 3),
        shifted(s2[:cut], "x", 1),
        shifted(s2[cut:], "x", 3),
    )
    s1, s3, s0 = joined(1), joined(2), joined(0)

    def added(block, term, at):
        total = lax.dynamic_slice_in_dim(block, at, cut, 0).astype(F32) + term.astype(F32)
        return lax.dynamic_update_slice_in_dim(block, total.astype(BF16), at, 0)

    f3, f1, e3, e1 = tied(
        shifted(added(g3, f1, 0), "y", 1),
        shifted(added(g1, f3, cut), "y", 3),
        shifted(added(s3, e1, 0), "x", 1),
        shifted(added(s1, e3, cut), "x", 3),
    )
    own0, own1 = packed(own, g0, f1, f3)
    other0, other1 = packed(other, s0, e1, e3)
    far, near, cross = tied(crossed(other0, 1, 0), crossed(own1, 0, 1), crossed(other1, 1, 1))
    flags = jnp.stack([t, m]).astype(jnp.int32)
    scale = (scale_factor / pairs).reshape(1)
    grad_proj = unpacked(flags, scale, [own0, far, near, cross], projected, inverse)

    loss_rows = loss_rows.reshape(4, part)
    loss_cols = loss_cols.reshape(2, 4, part)
    given = shifted(
        jnp.where(c == 0, jnp.stack([loss_rows, loss_rows]), loss_cols), "c", 1
    )
    losses = jnp.where(c == 0, loss_cols + given[::-1], jnp.stack([given[0], loss_rows]))
    losses, grad_proj = tied(losses, grad_proj)
    lines = losses.transpose(1, 0, 2).reshape(4, 1, rows)
    lines = jnp.pad(lines, ((0, 0), (0, 7), (0, half - rows)))

    grad_swap = shifted(grad_proj, "c", 1)
    weight_part = lax.dot_general(
        mine, grad_proj, (((0,), (0,)), ((), ())), preferred_element_type=F32
    ) + lax.dot_general(others, grad_swap, (((0,), (0,)), ((), ())), preferred_element_type=F32)

    small = half // 4
    lead = jnp.where(c == 0, x, y)
    back = jnp.where(c == 0, y, x)

    def message(k):
        block = pick(weight_part, (lead + k) % 4, small)
        return jnp.concatenate([block, lines[{0: 0, 1: 2, 2: 3, 3: 1}[k]]], axis=0)

    a2, a1, a3 = tied(*(turned(message(k), 0, k) for k in STEPS))
    piece = pick(weight_part, lead, small) + a1[:small] + a2[:small] + a3[:small]
    line = (lines[0] + a1[small:] + a2[small:] + a3[small:])[0, :rows].reshape(2, part)
    a2, a1, a3 = tied(*(turned(piece, 1, k) for k in STEPS))
    piece = (piece + a2) + (a1 + a3)
    given = shifted(jnp.where(c == 0, line[1], line[0]), "c", 1)
    loss_rows, loss_cols, piece = tied(
        jnp.where(c == 0, given, line[1]), jnp.where(c == 0, line[0], given), piece
    )
    pieces = [piece] + [turned(piece, 0, k) for k in (1, 3, 2)]
    loss_far = crossed(loss_cols, 1, 0)
    loss_near = crossed(jnp.where(m == 0, loss_rows, loss_far), 0, 1)
    upper = jnp.logical_and(t == 1, m == 1)
    lower = jnp.logical_and(t == 1, m == 0)
    row_loss = (
        jnp.where(lower, 0.0, loss_rows)
        + jnp.where(upper, 0.0, loss_far)
        + jnp.where(t == 1, loss_near, 0.0)
    ) / pairs
    *pieces, row_loss = tied(*pieces, row_loss)
    swapped = [shifted(v, "c", 1) for v in pieces]
    places = [c * half + (lead - k) % 4 * small for k in (0, 1, 3, 2)]
    places += [(1 - c) * half + (back - k) % 4 * small for k in (0, 1, 3, 2)]
    weight_grad = placed_rows(jnp.stack(places).astype(jnp.int32), pieces + swapped)
    return (row_loss[None], weight_grad[None])


def pack_kernel(embed_ref, *refs):
    out_refs = refs[3:]
    part, width = embed_ref.shape
    half = width // 2
    total = jnp.zeros((part, 128), F32)
    for k in range(2):
        here = pl.ds(k * half, half)
        grad = sum(ref[:, here].astype(F32) for ref in refs[:3])
        product = grad * embed_ref[:, here].astype(F32)
        total += sum(product[:, i * 128 : (i + 1) * 128] for i in range(half // 128))
        out_refs[k][:part, :] = grad.astype(BF16)
    line = jnp.sum(total.T, axis=0, keepdims=True)
    parts = []
    for _ in range(3):
        parts.append(line.astype(BF16).astype(F32))
        line = line - parts[-1]
    extra = jnp.broadcast_to(jnp.concatenate(parts, axis=1), (EXTRA, 3 * part)).astype(BF16)
    for k in range(2):
        out_refs[k][part:, :] = extra


def packed(embed, *grads):
    part, width = embed.shape
    vmem = pl.BlockSpec(memory_space=pltpu.VMEM)
    return pl.pallas_call(
        pack_kernel,
        in_specs=[vmem] * 4,
        out_specs=[vmem] * 2,
        out_shape=[jax.ShapeDtypeStruct((part + EXTRA, width // 2), BF16)] * 2,
        compiler_params=pltpu.CompilerParams(vmem_limit_bytes=32 * 2**20),
        cost_estimate=pl.CostEstimate(
            flops=6 * part * width, bytes_accessed=10 * part * width, transcendentals=0
        ),
    )(embed, *grads)


def unpack_kernel(flags_ref, scale_ref, p00, p10, p01, p11, projected_ref, inverse_ref, out_ref):
    part = p00.shape[0] - EXTRA
    t, m = flags_ref[0], flags_ref[1]
    scale = scale_ref[0]

    def finish(first, second, here):
        grad = first[:part, :].astype(F32) + second[:part, :].astype(F32)
        line = first[part : part + 1, :].astype(F32) + second[part : part + 1, :].astype(F32)
        line = line[:, :part] + line[:, part : 2 * part] + line[:, 2 * part :]
        along = jnp.broadcast_to(line, (128, part)).T[:, :1]
        inverse = inverse_ref[here, :]
        result = inverse * scale * (grad - inverse * along * projected_ref[here, :])
        out_ref[here, :] = result.astype(BF16)

    low, high = pl.ds(0, part), pl.ds(part, part)

    @pl.when(jnp.logical_and(t == 0, m == 0))
    def _():
        finish(p00, p10, low)
        finish(p01, p11, high)

    @pl.when(jnp.logical_and(t == 0, m == 1))
    def _():
        finish(p01, p11, low)
        finish(p00, p10, high)

    @pl.when(t == 1)
    def _():
        finish(p10, p11, low)
        finish(p00, p01, high)


def unpacked(flags, scale, pieces, projected, inverse):
    rows, half = projected.shape
    smem = pl.BlockSpec(memory_space=pltpu.SMEM)
    vmem = pl.BlockSpec(memory_space=pltpu.VMEM)
    return pl.pallas_call(
        unpack_kernel,
        in_specs=[smem] * 2 + [vmem] * 6,
        out_specs=vmem,
        out_shape=jax.ShapeDtypeStruct((rows, half), BF16),
        compiler_params=pltpu.CompilerParams(vmem_limit_bytes=32 * 2**20),
        cost_estimate=pl.CostEstimate(
            flops=6 * rows * half, bytes_accessed=10 * rows * half, transcendentals=0
        ),
    )(flags, scale, *pieces, projected, inverse)


def turned(value, late, step):
    route = []
    for i in range(32):
        x, y, c = i // 8, i // 2 % 4, i % 2
        if c ^ late:
            y = (y + step) % 4
        else:
            x = (x + step) % 4
        route.append((i, x * 8 + y * 2 + c))
    return lax.ppermute(value, ("x", "y", "c"), route)


def place_kernel(places_ref, *refs):
    *pieces, out_ref, sems = refs
    copies = []
    for i, ref in enumerate(pieces):
        size = ref.shape[0]
        here = pl.ds(pl.multiple_of(places_ref[i], size), size)
        copies.append(pltpu.make_async_copy(ref, out_ref.at[here, :], sems.at[i]))
        copies[-1].start()
    for copy in copies:
        copy.wait()


def placed_rows(places, pieces):
    size, width = pieces[0].shape
    anywhere = pl.BlockSpec(memory_space=pl.ANY)
    return pl.pallas_call(
        place_kernel,
        in_specs=[pl.BlockSpec(memory_space=pltpu.SMEM)] + [anywhere] * len(pieces),
        out_specs=anywhere,
        out_shape=jax.ShapeDtypeStruct((size * len(pieces), width), F32),
        scratch_shapes=[pltpu.SemaphoreType.DMA((len(pieces),))],
    )(places, *pieces)


def solution(mesh):
    fine = Mesh(mesh.devices.reshape(4, 4, 2, 2, 2), ("x", "y", "c", "m", "t"))
    dp = ("x", "y", "c")
    placed = (P("t", dp, None), P("t", None, "m"), P(), P())
    return jax.shard_map(
        on_device,
        mesh=fine,
        in_specs=placed,
        out_specs=(P("t", dp + ("m",)), P("t", None, "m")),
        check_vma=False,
    )
```

```python
import functools

import jax
import jax.numpy as jnp
from jax import lax
from jax.experimental import pallas as pl
from jax.experimental.pallas import tpu as pltpu
from jax.sharding import Mesh, PartitionSpec as P

F32 = jnp.float32
BF16 = jnp.bfloat16
STEPS = (2, 1, 3)
EXTRA = 16


def shifted(value, axis, step):
    count = lax.axis_size(axis)
    return lax.ppermute(value, axis, [(i, (i + step) % count) for i in range(count)])


def crossed(value, tower, half):
    flip = 2 * half + tower
    return lax.ppermute(value, ("m", "t"), [(i, i ^ flip) for i in range(4)])


def pick(block, index, size, axis=0):
    return lax.dynamic_slice_in_dim(block, index * size, size, axis)


def tied(*values):
    return lax.optimization_barrier(values)


def tile_kernel(n_rows, n_pairs, row_parts, col_parts, row_acc, col_acc, diagonal, *refs):
    refs = list(refs)
    diag_ref, scale_ref = refs.pop(0), refs.pop(0)

    def take(count):
        return [refs.pop(0) for _ in range(count)]

    rows_refs = [take(row_parts[r]) for r in range(n_rows)]
    cols_refs = [take(col_parts) for _ in range(2 * n_pairs)]
    row_sums = [take(1)[0] if row_acc[r] else None for r in range(n_rows)]
    col_sums = take(2 * n_pairs) if col_acc else None
    ga_refs, gb_refs = take(n_rows), take(2 * n_pairs)
    la_ref, lb_ref = take(2)
    acc_ref, loss_ref = take(2)
    part = loss_ref.shape[0] // n_rows
    width = acc_ref.shape[1]
    scale = scale_ref[0]
    bias = scale_ref[1]

    def block(parts):
        if len(parts) == 1:
            return parts[0][...]
        return jnp.concatenate([ref[...] for ref in parts], axis=0)

    for step in range(n_pairs):
        gb = [jnp.zeros((part, width), F32) for _ in range(2)]
        for r in range(n_rows):
            here = pl.ds(r * part, part)
            images = block(rows_refs[r])
            grad = jnp.zeros((part, width), F32)
            for core in range(2):
                texts = block(cols_refs[2 * step + core])
                logits = (
                    lax.dot_general(
                        images, texts, (((1,), (1,)), ((), ())), preferred_element_type=F32
                    )
                    * scale
                    + bias
                )
                meets = diagonal and step == 0 and r == 0 and core == 0
                if meets:
                    image = lax.broadcasted_iota(jnp.int32, (part, part), 0)
                    text = lax.broadcasted_iota(jnp.int32, (part, part), 1)
                    same = image + diag_ref[0] == text
                    logits = jnp.where(same, -logits, logits)
                grown = jnp.exp(logits)
                whole = 1.0 + grown
                inverse = 1.0 / whole
                losses = jnp.log(whole) + (grown - (whole - 1.0)) * inverse
                share = grown * inverse
                if meets:
                    share = jnp.where(same, -share, share)
                coefficient = share.astype(BF16)
                folded = sum(losses[:, k * 128 : (k + 1) * 128] for k in range(part // 128))
                column = jnp.sum(losses, axis=0, keepdims=True)
                if step == 0 and core == 0:
                    loss_ref[here, :] = folded
                else:
                    loss_ref[here, :] += folded
                if r == 0:
                    lb_ref[2 * step + core] = column
                else:
                    lb_ref[2 * step + core] += column
                grad += jnp.dot(coefficient, texts, preferred_element_type=F32)
                gb[core] += lax.dot_general(
                    coefficient, images, (((0,), (0,)), ((), ())), preferred_element_type=F32
                )
            if step == 0 and row_acc[r]:
                grad += row_sums[r][...]
            if step > 0:
                grad += acc_ref[here, :]
            if step < n_pairs - 1:
                acc_ref[here, :] = grad
            else:
                ga_refs[r][...] = grad.astype(ga_refs[r].dtype)
        for core in range(2):
            total = gb[core]
            if col_acc:
                total += col_sums[2 * step + core][...]
            gb_refs[2 * step + core][...] = total.astype(gb_refs[2 * step + core].dtype)
    for r in range(n_rows):
        la_ref[r] = jnp.sum(loss_ref[pl.ds(r * part, part), :].T, axis=0, keepdims=True)


def tile_terms(rows, cols, row_sums, col_sums, row_types, col_type, diagonal, diag, scales, grant):
    part = sum(v.shape[0] for v in rows[0])
    width = rows[0][0].shape[1]
    n_rows, n_pairs = len(rows), len(cols)
    smem = pl.BlockSpec(memory_space=pltpu.SMEM)
    vmem = pl.BlockSpec(memory_space=pltpu.VMEM)
    operands = [v for piece in rows for v in piece]
    operands += [v for pair in cols for piece in pair for v in piece]
    operands += [v for v in row_sums if v is not None] + list(col_sums or ())
    body = functools.partial(
        tile_kernel,
        n_rows,
        n_pairs,
        [len(piece) for piece in rows],
        len(cols[0][0]),
        [v is not None for v in row_sums],
        bool(col_sums),
        diagonal,
    )
    out_shape = [jax.ShapeDtypeStruct((part, width), kind) for kind in row_types]
    out_shape += [jax.ShapeDtypeStruct((part, width), col_type)] * (2 * n_pairs)
    out_shape += [jax.ShapeDtypeStruct((n, 1, part), F32) for n in (n_rows, 2 * n_pairs)]
    out = pl.pallas_call(
        body,
        in_specs=[smem, smem] + [vmem] * len(operands),
        out_specs=[vmem] * len(out_shape),
        out_shape=out_shape,
        scratch_shapes=[
            pltpu.VMEM((n_rows * part, width), F32),
            pltpu.VMEM((n_rows * part, 128), F32),
        ],
        compiler_params=pltpu.CompilerParams(vmem_limit_bytes=grant * 2**20),
        cost_estimate=pl.CostEstimate(
            flops=6 * n_rows * 2 * n_pairs * part * part * width,
            bytes_accessed=2 * 2 * (n_rows + 2 * n_pairs) * part * width,
            transcendentals=3 * 2 * n_rows * n_pairs * part * part,
        ),
    )(diag, scales, *operands)
    grad_rows, grad_cols = out[:n_rows], out[n_rows : n_rows + 2 * n_pairs]
    return grad_rows, grad_cols, out[-2].reshape(n_rows, part), out[-1].reshape(n_pairs, 2, part)


def on_device(features, projection, similarity_scale, logit_bias):
    x, y, c = lax.axis_index("x"), lax.axis_index("y"), lax.axis_index("c")
    m, t = lax.axis_index("m"), lax.axis_index("t")
    inputs = features[0]
    rows, width = inputs.shape
    weight = projection[0]
    half = weight.shape[1]
    part = rows // 2
    pairs = rows * 32
    scale_factor = similarity_scale[0]

    projected = jnp.dot(inputs, weight, preferred_element_type=F32)
    squares = lax.psum(jnp.sum(projected * projected, axis=1), "m")[:, None]
    inverse = lax.rsqrt(squares + 1e-06)
    embedded = (projected * inverse).astype(BF16)
    mine = pick(inputs, c, half, 1)
    others = shifted(pick(inputs, 1 - c, half, 1), "c", 1)

    def rows_for(tower, flip):
        return pick(embedded, jnp.where(t == 0, m ^ flip, 1 ^ tower), part)

    kept = rows_for(0, 0)
    far, near, cross = tied(
        crossed(rows_for(1, 0), 1, 0), crossed(rows_for(0, 1), 0, 1), crossed(rows_for(1, 1), 1, 1)
    )
    own = jnp.concatenate([kept, near], axis=1)
    other = jnp.concatenate([far, cross], axis=1)
    own, other = tied(own, other)

    cut = part // 2
    r1, r3, c1, c3, d0 = tied(
        shifted(own, "y", 1),
        shifted(own, "y", 3),
        shifted(other, "x", 1),
        shifted(other, "x", 3),
        shifted(other, "c", 1),
    )
    c2a, c2b, r2a, r2b = (
        shifted(c1[:cut], "x", 1),
        shifted(c3[cut:], "x", 3),
        shifted(r1[:cut], "y", 1),
        shifted(r3[cut:], "y", 3),
    )
    d1, d3 = shifted(c1, "c", 1), shifted(c3, "c", 1)
    diag = jnp.where(m == t, 0, 2 * part).astype(jnp.int32).reshape(1)
    scales = jnp.stack([scale_factor, logit_bias[0]])
    near_rows = [[own], [r1], [r3]]
    near_cols = [[[other], [d0]], [[c1], [d1]], [[c3], [d3]]]
    rows_sum, cols_sum, la, lb = tile_terms(
        near_rows, near_cols, [None] * 3, None, [F32] * 3, F32, True, diag, scales, 30
    )
    c2a, c2b, r2a, r2b, rows_sum, cols_sum = tied(c2a, c2b, r2a, r2b, rows_sum, cols_sum)
    d2a, d2b = shifted(c2a, "c", 1), shifted(c2b, "c", 1)
    (g0, g1, g3, sum2), far_cols, la2, lb2 = tile_terms(
        near_rows + [[r2a, r2b]],
        [[[c2a, c2b], [d2a, d2b]]],
        list(rows_sum) + [None],
        None,
        [BF16] * 3 + [F32],
        BF16,
        False,
        diag,
        scales,
        24,
    )
    given = shifted(far_cols[1], "c", 1)
    s2 = (far_cols[0].astype(F32) + given.astype(F32)).astype(BF16)
    (g2,), grad_cols, la3, lb3 = tile_terms(
        [[r2a, r2b]], near_cols, [sum2], cols_sum, [BF16], BF16, False, diag, scales, 30
    )
    e1, e3 = shifted(s2[:cut], "x", 1), shifted(s2[cut:], "x", 3)
    f1, f3 = shifted(g2[:cut], "y", 1), shifted(g2[cut:], "y", 3)
    loss_rows = jnp.concatenate([la + la2[:3], la2[3:] + la3])
    loss_cols = jnp.concatenate([lb + lb3, lb2]).transpose(1, 0, 2)

    def joined(k):
        given = shifted(grad_cols[2 * k + 1], "c", 1)
        return (grad_cols[2 * k].astype(F32) + given.astype(F32)).astype(BF16)

    s1, s3, s0 = joined(1), joined(2), joined(0)

    def added(block, term, at):
        total = lax.dynamic_slice_in_dim(block, at, cut, 0).astype(F32) + term.astype(F32)
        return lax.dynamic_update_slice_in_dim(block, total.astype(BF16), at, 0)

    e3, e1 = shifted(added(s3, e1, 0), "x", 1), shifted(added(s1, e3, cut), "x", 3)
    f3, f1 = shifted(added(g3, f1, 0), "y", 1), shifted(added(g1, f3, cut), "y", 3)
    e1, e3, f1, f3 = tied(e1, e3, f1, f3)
    own0, own1 = packed(own, g0, f1, f3)
    other0, other1 = packed(other, s0, e1, e3)
    far, near, cross = tied(crossed(other0, 1, 0), crossed(own1, 0, 1), crossed(other1, 1, 1))
    flags = jnp.stack([t, m]).astype(jnp.int32)
    scale = (scale_factor / pairs).reshape(1)
    grad_proj = unpacked(flags, scale, [own0, far, near, cross], projected, inverse)

    given = shifted(
        jnp.where(c == 0, jnp.stack([loss_rows, loss_rows]), loss_cols), "c", 1
    )
    losses = jnp.where(c == 0, loss_cols + given[::-1], jnp.stack([given[0], loss_rows]))
    losses, grad_proj = tied(losses, grad_proj)
    lines = losses.transpose(1, 0, 2).reshape(4, 1, rows)
    lines = jnp.pad(lines, ((0, 0), (0, 7), (0, half - rows)))

    grad_swap = shifted(grad_proj, "c", 1)
    weight_part = lax.dot_general(
        mine, grad_proj, (((0,), (0,)), ((), ())), preferred_element_type=F32
    ) + lax.dot_general(others, grad_swap, (((0,), (0,)), ((), ())), preferred_element_type=F32)

    small = half // 4
    lead = jnp.where(c == 0, x, y)
    back = jnp.where(c == 0, y, x)

    def message(k):
        block = pick(weight_part, (lead + k) % 4, small)
        return jnp.concatenate([block, lines[{0: 0, 1: 2, 2: 3, 3: 1}[k]]], axis=0)

    a2, a1, a3 = tied(*(turned(message(k), 0, k) for k in STEPS))
    piece = pick(weight_part, lead, small) + a1[:small] + a2[:small] + a3[:small]
    line = (lines[0] + a1[small:] + a2[small:] + a3[small:])[0, :rows].reshape(2, part)
    a2, a1, a3 = tied(*(turned(piece, 1, k) for k in STEPS))
    piece = (piece + a2) + (a1 + a3)
    given = shifted(jnp.where(c == 0, line[1], line[0]), "c", 1)
    loss_rows, loss_cols, piece = tied(
        jnp.where(c == 0, given, line[1]), jnp.where(c == 0, line[0], given), piece
    )
    pieces = [piece] + [turned(piece, 0, k) for k in (1, 3, 2)]
    loss_far = crossed(loss_cols, 1, 0)
    loss_near = crossed(jnp.where(m == 0, loss_rows, loss_far), 0, 1)
    upper = jnp.logical_and(t == 1, m == 1)
    lower = jnp.logical_and(t == 1, m == 0)
    row_loss = (
        jnp.where(lower, 0.0, loss_rows)
        + jnp.where(upper, 0.0, loss_far)
        + jnp.where(t == 1, loss_near, 0.0)
    ) / pairs
    *pieces, row_loss = tied(*pieces, row_loss)
    swapped = [shifted(v, "c", 1) for v in pieces]
    places = [c * half + (lead - k) % 4 * small for k in (0, 1, 3, 2)]
    places += [(1 - c) * half + (back - k) % 4 * small for k in (0, 1, 3, 2)]
    weight_grad = placed_rows(jnp.stack(places).astype(jnp.int32), pieces + swapped)
    return (row_loss[None], weight_grad[None])


def pack_kernel(embed_ref, *refs):
    out_refs = refs[3:]
    part, width = embed_ref.shape
    half = width // 2
    total = jnp.zeros((part, 128), F32)
    for k in range(2):
        here = pl.ds(k * half, half)
        grad = sum(ref[:, here].astype(F32) for ref in refs[:3])
        product = grad * embed_ref[:, here].astype(F32)
        total += sum(product[:, i * 128 : (i + 1) * 128] for i in range(half // 128))
        out_refs[k][:part, :] = grad.astype(BF16)
    line = jnp.sum(total.T, axis=0, keepdims=True)
    parts = []
    for _ in range(3):
        parts.append(line.astype(BF16).astype(F32))
        line = line - parts[-1]
    extra = jnp.broadcast_to(jnp.concatenate(parts, axis=1), (EXTRA, 3 * part)).astype(BF16)
    for k in range(2):
        out_refs[k][part:, :] = extra


def packed(embed, *grads):
    part, width = embed.shape
    vmem = pl.BlockSpec(memory_space=pltpu.VMEM)
    return pl.pallas_call(
        pack_kernel,
        in_specs=[vmem] * 4,
        out_specs=[vmem] * 2,
        out_shape=[jax.ShapeDtypeStruct((part + EXTRA, width // 2), BF16)] * 2,
        compiler_params=pltpu.CompilerParams(vmem_limit_bytes=12 * 2**20),
        cost_estimate=pl.CostEstimate(
            flops=6 * part * width, bytes_accessed=10 * part * width, transcendentals=0
        ),
    )(embed, *grads)


def unpack_kernel(flags_ref, scale_ref, p00, p10, p01, p11, projected_ref, inverse_ref, out_ref):
    part = p00.shape[0] - EXTRA
    t, m = flags_ref[0], flags_ref[1]
    scale = scale_ref[0]

    def finish(first, second, here):
        grad = first[:part, :].astype(F32) + second[:part, :].astype(F32)
        line = first[part : part + 1, :].astype(F32) + second[part : part + 1, :].astype(F32)
        line = line[:, :part] + line[:, part : 2 * part] + line[:, 2 * part :]
        along = jnp.broadcast_to(line, (128, part)).T[:, :1]
        inverse = inverse_ref[here, :]
        result = inverse * scale * (grad - inverse * along * projected_ref[here, :])
        out_ref[here, :] = result.astype(BF16)

    low, high = pl.ds(0, part), pl.ds(part, part)

    @pl.when(jnp.logical_and(t == 0, m == 0))
    def _():
        finish(p00, p10, low)
        finish(p01, p11, high)

    @pl.when(jnp.logical_and(t == 0, m == 1))
    def _():
        finish(p01, p11, low)
        finish(p00, p10, high)

    @pl.when(t == 1)
    def _():
        finish(p10, p11, low)
        finish(p00, p01, high)


def unpacked(flags, scale, pieces, projected, inverse):
    rows, half = projected.shape
    smem = pl.BlockSpec(memory_space=pltpu.SMEM)
    vmem = pl.BlockSpec(memory_space=pltpu.VMEM)
    return pl.pallas_call(
        unpack_kernel,
        in_specs=[smem] * 2 + [vmem] * 6,
        out_specs=vmem,
        out_shape=jax.ShapeDtypeStruct((rows, half), BF16),
        compiler_params=pltpu.CompilerParams(vmem_limit_bytes=12 * 2**20),
        cost_estimate=pl.CostEstimate(
            flops=6 * rows * half, bytes_accessed=10 * rows * half, transcendentals=0
        ),
    )(flags, scale, *pieces, projected, inverse)


def turned(value, late, step):
    route = []
    for i in range(32):
        x, y, c = i // 8, i // 2 % 4, i % 2
        if c ^ late:
            y = (y + step) % 4
        else:
            x = (x + step) % 4
        route.append((i, x * 8 + y * 2 + c))
    return lax.ppermute(value, ("x", "y", "c"), route)


def place_kernel(places_ref, *refs):
    *pieces, out_ref, sems = refs
    copies = []
    for i, ref in enumerate(pieces):
        size = ref.shape[0]
        here = pl.ds(pl.multiple_of(places_ref[i], size), size)
        copies.append(pltpu.make_async_copy(ref, out_ref.at[here, :], sems.at[i]))
        copies[-1].start()
    for copy in copies:
        copy.wait()


def placed_rows(places, pieces):
    size, width = pieces[0].shape
    vmem = pl.BlockSpec(memory_space=pltpu.VMEM)
    return pl.pallas_call(
        place_kernel,
        in_specs=[pl.BlockSpec(memory_space=pltpu.SMEM)] + [vmem] * len(pieces),
        out_specs=pl.BlockSpec(memory_space=pl.ANY),
        out_shape=jax.ShapeDtypeStruct((size * len(pieces), width), F32),
        scratch_shapes=[pltpu.SemaphoreType.DMA((len(pieces),))],
        compiler_params=pltpu.CompilerParams(vmem_limit_bytes=8 * 2**20),
    )(places, *pieces)


def solution(mesh):
    fine = Mesh(mesh.devices.reshape(4, 4, 2, 2, 2), ("x", "y", "c", "m", "t"))
    dp = ("x", "y", "c")
    placed = (P("t", dp, None), P("t", None, "m"), P(), P())
    return jax.shard_map(
        on_device,
        mesh=fine,
        in_specs=placed,
        out_specs=(P("t", dp + ("m",)), P("t", None, "m")),
        check_vma=False,
    )
```

```python
import functools

import jax
import jax.numpy as jnp
from jax import lax
from jax.experimental import pallas as pl
from jax.experimental.pallas import tpu as pltpu
from jax.sharding import Mesh, PartitionSpec as P

F32 = jnp.float32
BF16 = jnp.bfloat16
STEPS = (2, 1, 3)
EXTRA = 16


def shifted(value, axis, step):
    count = lax.axis_size(axis)
    return lax.ppermute(value, axis, [(i, (i + step) % count) for i in range(count)])


def crossed(value, tower, half):
    flip = 2 * half + tower
    return lax.ppermute(value, ("m", "t"), [(i, i ^ flip) for i in range(4)])


def pick(block, index, size, axis=0):
    return lax.dynamic_slice_in_dim(block, index * size, size, axis)


def tied(*values):
    return lax.optimization_barrier(values)


def in_hbm(values):
    return [pltpu.with_memory_space_constraint(v, pltpu.HBM) for v in values]


def tile_kernel(row_acc, col_acc, row_types, diagonal, *refs):
    refs = list(refs)
    n_rows, n_pairs = len(row_acc), len(col_acc)

    def take(count):
        return [refs.pop(0) for _ in range(count)]

    diag_ref, scale_ref = take(2)
    rows_refs = take(n_rows)
    cols_refs = [take(2) for _ in range(n_pairs)]
    row_sums = [refs.pop(0) if has else None for has in row_acc]
    col_sums = [take(2) if has else None for has in col_acc]
    ga_refs, gb_refs = take(n_rows), take(2 * n_pairs)
    la_ref, lb_ref, acc_ref, loss_ref = take(4)
    part, width = rows_refs[0].shape
    scale = scale_ref[0]
    bias = scale_ref[1]

    for step in range(n_pairs):
        gb = [jnp.zeros((part, width), F32) for _ in range(2)]
        for r in range(n_rows):
            here = pl.ds(r * part, part)
            images = rows_refs[r][...]
            grad = jnp.zeros((part, width), F32)
            for core in range(2):
                texts = cols_refs[step][core][...]
                logits = (
                    lax.dot_general(
                        images, texts, (((1,), (1,)), ((), ())), preferred_element_type=F32
                    )
                    * scale
                    + bias
                )
                meets = diagonal and step == 0 and r == 0 and core == 0
                if meets:
                    image = lax.broadcasted_iota(jnp.int32, (part, part), 0)
                    text = lax.broadcasted_iota(jnp.int32, (part, part), 1)
                    same = image + diag_ref[0] == text
                    logits = jnp.where(same, -logits, logits)
                grown = jnp.exp(logits)
                whole = 1.0 + grown
                inverse = 1.0 / whole
                losses = jnp.log(whole) + (grown - (whole - 1.0)) * inverse
                share = grown * inverse
                if meets:
                    share = jnp.where(same, -share, share)
                coefficient = share.astype(BF16)
                folded = sum(losses[:, k * 128 : (k + 1) * 128] for k in range(part // 128))
                column = jnp.sum(losses, axis=0, keepdims=True)
                if step == 0 and core == 0:
                    loss_ref[here, :] = folded
                else:
                    loss_ref[here, :] += folded
                if r == 0:
                    lb_ref[2 * step + core] = column
                else:
                    lb_ref[2 * step + core] += column
                grad += jnp.dot(coefficient, texts, preferred_element_type=F32)
                gb[core] += lax.dot_general(
                    coefficient, images, (((0,), (0,)), ((), ())), preferred_element_type=F32
                )
            if step == 0 and row_acc[r]:
                grad += row_sums[r][...]
            if step > 0:
                grad += acc_ref[here, :]
            if step < n_pairs - 1:
                acc_ref[here, :] = grad
            else:
                ga_refs[r][...] = grad.astype(row_types[r])
        for core in range(2):
            total = gb[core]
            if col_acc[step]:
                total += col_sums[step][core][...]
            gb_refs[2 * step + core][...] = total.astype(gb_refs[2 * step + core].dtype)
    for r in range(n_rows):
        la_ref[r] = jnp.sum(loss_ref[pl.ds(r * part, part), :].T, axis=0, keepdims=True)


def tile_terms(rows, cols, row_sums, col_sums, row_types, col_types, diagonal, diag, scales):
    part, width = rows[0].shape
    n_rows, n_pairs = len(rows), len(cols)
    smem = pl.BlockSpec(memory_space=pltpu.SMEM)
    vmem = pl.BlockSpec(memory_space=pltpu.VMEM)
    operands = in_hbm(list(rows) + [v for pair in cols for v in pair])
    operands += [v for v in row_sums if v is not None]
    operands += [v for pair in col_sums if pair is not None for v in pair]
    body = functools.partial(
        tile_kernel,
        [v is not None for v in row_sums],
        [v is not None for v in col_sums],
        row_types,
        diagonal,
    )
    kinds = list(row_types) + [kind for kind in col_types for _ in range(2)]
    out_shape = [
        jax.ShapeDtypeStruct((part, width), F32) if kind == F32 else pltpu.HBM((part, width), kind)
        for kind in kinds
    ]
    n_out = len(out_shape)
    out_shape += [jax.ShapeDtypeStruct((n, 1, part), F32) for n in (n_rows, 2 * n_pairs)]
    out = pl.pallas_call(
        body,
        in_specs=[smem, smem] + [vmem] * len(operands),
        out_specs=[vmem] * len(out_shape),
        out_shape=out_shape,
        scratch_shapes=[
            pltpu.VMEM((n_rows * part if n_pairs > 1 else 8, width), F32),
            pltpu.VMEM((n_rows * part, 128), F32),
        ],
        compiler_params=pltpu.CompilerParams(vmem_limit_bytes=32 * 2**20),
        cost_estimate=pl.CostEstimate(
            flops=6 * n_rows * 2 * n_pairs * part * part * width,
            bytes_accessed=2 * 2 * (n_rows + 2 * n_pairs) * part * width,
            transcendentals=3 * 2 * n_rows * n_pairs * part * part,
        ),
    )(diag, scales, *operands)
    grad_rows, grad_cols = out[:n_rows], out[n_rows:n_out]
    return grad_rows, grad_cols, out[-2].reshape(n_rows, part), out[-1].reshape(n_pairs, 2, part)


def staged(body, smalls, operands, out_shape, cost):
    vmem = pl.BlockSpec(memory_space=pltpu.VMEM)
    return pl.pallas_call(
        body,
        in_specs=[pl.BlockSpec(memory_space=pltpu.SMEM)] * len(smalls) + [vmem] * len(operands),
        out_specs=jax.tree.map(lambda _: vmem, out_shape),
        out_shape=out_shape,
        compiler_params=pltpu.CompilerParams(vmem_limit_bytes=10 * 2**20),
        cost_estimate=pl.CostEstimate(flops=cost, bytes_accessed=2 * cost, transcendentals=0),
    )(*smalls, *in_hbm(operands))


def on_device(features, projection, similarity_scale, logit_bias):
    x, y, c = lax.axis_index("x"), lax.axis_index("y"), lax.axis_index("c")
    m, t = lax.axis_index("m"), lax.axis_index("t")
    inputs = features[0]
    rows, width = inputs.shape
    weight = projection[0]
    half = weight.shape[1]
    part = rows // 2
    pairs = rows * 32
    scale_factor = similarity_scale[0]

    projected = jnp.dot(inputs, weight, preferred_element_type=F32)
    squares = lax.psum(jnp.sum(projected * projected, axis=1), "m")[:, None]
    inverse = lax.rsqrt(squares + 1e-06)
    embedded = (projected * inverse).astype(BF16)
    mine = pick(inputs, c, half, 1)
    others = shifted(pick(inputs, 1 - c, half, 1), "c", 1)

    def rows_for(tower, flip):
        return pick(embedded, jnp.where(t == 0, m ^ flip, 1 ^ tower), part)

    kept = rows_for(0, 0)
    far, near, cross = tied(
        crossed(rows_for(1, 0), 1, 0), crossed(rows_for(0, 1), 0, 1), crossed(rows_for(1, 1), 1, 1)
    )
    own = jnp.concatenate([kept, near], axis=1)
    other = jnp.concatenate([far, cross], axis=1)
    own, other = tied(own, other)

    r1, r3, c1, c3, d0 = tied(
        shifted(own, "y", 1),
        shifted(own, "y", 3),
        shifted(other, "x", 1),
        shifted(other, "x", 3),
        shifted(other, "c", 1),
    )
    c2, r2 = shifted(other, "x", 2), shifted(own, "y", 2)
    d1, d3 = shifted(c1, "c", 1), shifted(c3, "c", 1)
    diag = jnp.where(m == t, 0, 2 * part).astype(jnp.int32).reshape(1)
    scales = jnp.stack([scale_factor, logit_bias[0]])
    near = [own, r1, r3]
    cols0, cols1, cols3 = [other, d0], [c1, d1], [c3, d3]
    rows_sum, (a0, b0, a1, b1, a3, b3), la, lb = tile_terms(
        near,
        [cols0, cols1, cols3],
        [None] * 3,
        [None] * 3,
        [F32] * 3,
        [F32] * 3,
        True,
        diag,
        scales,
    )
    c2, r2, a0, b0, a1, b1, a3, b3, *rows_sum = tied(c2, r2, a0, b0, a1, b1, a3, b3, *rows_sum)
    d2 = shifted(c2, "c", 1)
    (sum2,), (s1, t1, s3, t3), la2, lb2 = tile_terms(
        [r2], [cols1, cols3], [None], [[a1, b1], [a3, b3]], [F32], [BF16] * 2, False, diag, scales
    )
    t1, t3 = shifted(t1, "c", 1), shifted(t3, "c", 1)
    (g2,), (s0, t0, a2, b2), la4, lb4 = tile_terms(
        [r2], [cols0, [c2, d2]], [sum2], [[a0, b0], None], [BF16], [BF16, F32], False, diag, scales
    )
    t1, t3, g2, s0, t0, a2, b2 = tied(t1, t3, g2, s0, t0, a2, b2)

    def joined(a, b):
        return (a.astype(F32) + b.astype(F32)).astype(BF16)

    s1, s3, a2, b2 = tied(joined(s1, t1), joined(s3, t3), a2, b2)
    e1, e3 = shifted(s1, "x", 3), shifted(s3, "x", 1)
    f2 = shifted(g2, "y", 2)
    t0 = shifted(t0, "c", 1)
    (g0, g1, g3), (s2, t2), la3, lb3 = tile_terms(
        near, [[c2, d2]], rows_sum, [[a2, b2]], [BF16] * 3, [BF16], False, diag, scales
    )
    loss_rows = jnp.concatenate([la + la3, la2 + la4])
    loss_cols = jnp.stack([lb[0] + lb4[0], lb[1] + lb2[0], lb[2] + lb2[1], lb4[1] + lb3[0]], axis=1)
    e1, e3, f2, t0, g0, g1, g3, s2, t2 = tied(e1, e3, f2, t0, g0, g1, g3, s2, t2)
    s2 = joined(s2, shifted(t2, "c", 1))
    f1, f3 = shifted(g1, "y", 3), shifted(g3, "y", 1)
    e2 = shifted(s2, "x", 2)
    e2, f1, f3 = tied(e2, f1, f3)
    own0, own1 = packed(own, g0, f1, f2, f3)
    other0, other1 = packed(other, s0, t0, e1, e2, e3)
    far, near, cross = tied(crossed(other0, 1, 0), crossed(own1, 0, 1), crossed(other1, 1, 1))
    flags = jnp.stack([t, m]).astype(jnp.int32)
    scale = (scale_factor / pairs).reshape(1)
    grad_proj = unpacked(flags, scale, [own0, far, near, cross], projected, inverse)

    given = shifted(
        jnp.where(c == 0, jnp.stack([loss_rows, loss_rows]), loss_cols), "c", 1
    )
    losses = jnp.where(c == 0, loss_cols + given[::-1], jnp.stack([given[0], loss_rows]))
    losses, grad_proj = tied(losses, grad_proj)
    lines = losses.transpose(1, 0, 2).reshape(4, 1, rows)
    lines = jnp.pad(lines, ((0, 0), (0, 7), (0, half - rows)))

    grad_swap = shifted(grad_proj, "c", 1)
    weight_part = lax.dot_general(
        mine, grad_proj, (((0,), (0,)), ((), ())), preferred_element_type=F32
    ) + lax.dot_general(others, grad_swap, (((0,), (0,)), ((), ())), preferred_element_type=F32)

    small = half // 4
    lead = jnp.where(c == 0, x, y)
    back = jnp.where(c == 0, y, x)

    def message(k):
        block = pick(weight_part, (lead + k) % 4, small)
        return jnp.concatenate([block, lines[{0: 0, 1: 2, 2: 3, 3: 1}[k]]], axis=0)

    a2, a1, a3 = tied(*(turned(message(k), 0, k) for k in STEPS))
    piece = pick(weight_part, lead, small) + a1[:small] + a2[:small] + a3[:small]
    line = (lines[0] + a1[small:] + a2[small:] + a3[small:])[0, :rows].reshape(2, part)
    a2, a1, a3 = tied(*(turned(piece, 1, k) for k in STEPS))
    piece = (piece + a2) + (a1 + a3)
    given = shifted(jnp.where(c == 0, line[1], line[0]), "c", 1)
    loss_rows, loss_cols, piece = tied(
        jnp.where(c == 0, given, line[1]), jnp.where(c == 0, line[0], given), piece
    )
    pieces = [piece] + [turned(piece, 0, k) for k in (1, 3, 2)]
    loss_far = crossed(loss_cols, 1, 0)
    loss_near = crossed(jnp.where(m == 0, loss_rows, loss_far), 0, 1)
    upper = jnp.logical_and(t == 1, m == 1)
    lower = jnp.logical_and(t == 1, m == 0)
    row_loss = (
        jnp.where(lower, 0.0, loss_rows)
        + jnp.where(upper, 0.0, loss_far)
        + jnp.where(t == 1, loss_near, 0.0)
    ) / pairs
    *pieces, row_loss = tied(*pieces, row_loss)
    swapped = [shifted(v, "c", 1) for v in pieces]
    places = [c * half + (lead - k) % 4 * small for k in (0, 1, 3, 2)]
    places += [(1 - c) * half + (back - k) % 4 * small for k in (0, 1, 3, 2)]
    weight_grad = placed_rows(jnp.stack(places).astype(jnp.int32), pieces + swapped)
    return (row_loss[None], weight_grad[None])


def pack_kernel(embed_ref, *refs):
    refs, out_refs = refs[:-2], refs[-2:]
    part, width = embed_ref.shape
    half = width // 2
    total = jnp.zeros((part, 128), F32)
    for k in range(2):
        here = pl.ds(k * half, half)
        grad = sum(ref[:, here].astype(F32) for ref in refs)
        product = grad * embed_ref[:, here].astype(F32)
        total += sum(product[:, i * 128 : (i + 1) * 128] for i in range(half // 128))
        out_refs[k][:part, :] = grad.astype(BF16)
    line = jnp.sum(total.T, axis=0, keepdims=True)
    parts = []
    for _ in range(3):
        parts.append(line.astype(BF16).astype(F32))
        line = line - parts[-1]
    extra = jnp.broadcast_to(jnp.concatenate(parts, axis=1), (EXTRA, 3 * part)).astype(BF16)
    for k in range(2):
        out_refs[k][part:, :] = extra


def packed(embed, *grads):
    part, width = embed.shape
    out = [pltpu.HBM((part + EXTRA, width // 2), BF16)] * 2
    return staged(pack_kernel, (), (embed,) + grads, out, 6 * part * width)


def unpack_kernel(flags_ref, scale_ref, p00, p10, p01, p11, projected_ref, inverse_ref, out_ref):
    part = p00.shape[0] - EXTRA
    t, m = flags_ref[0], flags_ref[1]
    scale = scale_ref[0]

    def finish(first, second, here):
        grad = first[:part, :].astype(F32) + second[:part, :].astype(F32)
        line = first[part : part + 1, :].astype(F32) + second[part : part + 1, :].astype(F32)
        line = line[:, :part] + line[:, part : 2 * part] + line[:, 2 * part :]
        along = jnp.broadcast_to(line, (128, part)).T[:, :1]
        inverse = inverse_ref[here, :]
        result = inverse * scale * (grad - inverse * along * projected_ref[here, :])
        out_ref[here, :] = result.astype(BF16)

    low, high = pl.ds(0, part), pl.ds(part, part)

    @pl.when(jnp.logical_and(t == 0, m == 0))
    def _():
        finish(p00, p10, low)
        finish(p01, p11, high)

    @pl.when(jnp.logical_and(t == 0, m == 1))
    def _():
        finish(p01, p11, low)
        finish(p00, p10, high)

    @pl.when(t == 1)
    def _():
        finish(p10, p11, low)
        finish(p00, p01, high)


def unpacked(flags, scale, pieces, projected, inverse):
    out = jax.ShapeDtypeStruct(projected.shape, BF16)
    operands = (*pieces, projected, inverse)
    return staged(unpack_kernel, (flags, scale), operands, out, 6 * projected.size)


def turned(value, late, step):
    route = []
    for i in range(32):
        x, y, c = i // 8, i // 2 % 4, i % 2
        if c ^ late:
            y = (y + step) % 4
        else:
            x = (x + step) % 4
        route.append((i, x * 8 + y * 2 + c))
    return lax.ppermute(value, ("x", "y", "c"), route)


def place_kernel(places_ref, *refs):
    *pieces, out_ref, sems = refs
    copies = []
    for i, piece in enumerate(pieces):
        size = piece.shape[0]
        here = pl.ds(pl.multiple_of(places_ref[i], size), size)
        copies.append(pltpu.make_async_copy(piece, out_ref.at[here, :], sems.at[i]))
        copies[-1].start()
    for copy in copies:
        copy.wait()


def placed_rows(places, pieces):
    size, width = pieces[0].shape
    count = len(pieces)
    return pl.pallas_call(
        place_kernel,
        in_specs=[pl.BlockSpec(memory_space=pltpu.SMEM)]
        + [pl.BlockSpec(memory_space=pltpu.VMEM)] * count,
        out_specs=pl.BlockSpec(memory_space=pltpu.HBM),
        out_shape=pltpu.HBM((size * count, width), F32),
        scratch_shapes=[pltpu.SemaphoreType.DMA((count,))],
        compiler_params=pltpu.CompilerParams(vmem_limit_bytes=10 * 2**20),
    )(places, *in_hbm(pieces))


def solution(mesh):
    fine = Mesh(mesh.devices.reshape(4, 4, 2, 2, 2), ("x", "y", "c", "m", "t"))
    dp = ("x", "y", "c")
    placed = (P("t", dp, None), P("t", None, "m"), P(), P())
    return jax.shard_map(
        on_device,
        mesh=fine,
        in_specs=placed,
        out_specs=(P("t", dp + ("m",)), P("t", None, "m")),
        check_vma=False,
    )
```

```python
import functools
import math

import jax
import jax.numpy as jnp
from jax import lax
from jax.experimental import pallas as pl
from jax.experimental.pallas import tpu as pltpu
from jax.sharding import Mesh, PartitionSpec as P

F32 = jnp.float32
BF16 = jnp.bfloat16
STEPS = (2, 1, 3)
EXTRA = 16


def shifted(value, axis, step):
    count = lax.axis_size(axis)
    return lax.ppermute(value, axis, [(i, (i + step) % count) for i in range(count)])


def crossed(value, tower, half):
    flip = 2 * half + tower
    return lax.ppermute(value, ("m", "t"), [(i, i ^ flip) for i in range(4)])


def pick(block, index, size, axis=0):
    return lax.dynamic_slice_in_dim(block, index * size, size, axis)


def tied(*values):
    return lax.optimization_barrier(values)


def in_hbm(values):
    return [pltpu.with_memory_space_constraint(v, pltpu.HBM) for v in values]


def tile_kernel(row_acc, col_acc, row_types, diagonal, *refs):
    refs = list(refs)
    n_rows, n_pairs = len(row_acc), len(col_acc)

    def take(count):
        return [refs.pop(0) for _ in range(count)]

    diag_ref, scale_ref = take(2)
    rows_refs = take(n_rows)
    cols_refs = [take(2) for _ in range(n_pairs)]
    row_sums = [refs.pop(0) if has else None for has in row_acc]
    col_sums = [take(2) if has else None for has in col_acc]
    ga_refs, gb_refs = take(n_rows), take(2 * n_pairs)
    la_ref, lb_ref, acc_ref, loss_ref = take(4)
    part, width = rows_refs[0].shape
    scale = scale_ref[0]
    bias = scale_ref[1]

    def products(step, r, core):
        return lax.dot_general(
            rows_refs[r][...],
            cols_refs[step][core][...],
            (((1,), (1,)), ((), ())),
            preferred_element_type=F32,
        )

    order = [(k, r, core) for k in range(n_pairs) for r in range(n_rows) for core in range(2)]
    coming = products(*order[0])
    for i, (step, r, core) in enumerate(order):
        logits = coming * scale + bias
        if i + 1 < len(order):
            coming = products(*order[i + 1])
        here = pl.ds(r * part, part)
        if r == 0 and core == 0:
            gb = [jnp.zeros((part, width), F32) for _ in range(2)]
        if core == 0:
            grad = jnp.zeros((part, width), F32)
        meets = diagonal and i == 0
        if meets:
            image = lax.broadcasted_iota(jnp.int32, (part, part), 0)
            text = lax.broadcasted_iota(jnp.int32, (part, part), 1)
            same = image + diag_ref[0] == text
            logits = jnp.where(same, -logits, logits)
        grown = jnp.exp2(logits)
        whole = 1.0 + grown
        inverse = pl.reciprocal(whole, approx=True)
        inverse = inverse * (2.0 - whole * inverse)
        losses = jnp.log(whole) + (grown - (whole - 1.0)) * inverse
        share = grown * inverse
        if meets:
            share = jnp.where(same, -share, share)
        coefficient = share.astype(BF16)
        folded = sum(losses[:, k * 128 : (k + 1) * 128] for k in range(part // 128))
        column = jnp.sum(losses, axis=0, keepdims=True)
        if step == 0 and core == 0:
            loss_ref[here, :] = folded
        else:
            loss_ref[here, :] += folded
        if r == 0:
            lb_ref[2 * step + core] = column
        else:
            lb_ref[2 * step + core] += column
        grad += jnp.dot(coefficient, cols_refs[step][core][...], preferred_element_type=F32)
        gb[core] += lax.dot_general(
            coefficient, rows_refs[r][...], (((0,), (0,)), ((), ())), preferred_element_type=F32
        )
        if core == 1:
            if step == 0 and row_acc[r]:
                grad += row_sums[r][...]
            if step > 0:
                grad += acc_ref[here, :]
            if step < n_pairs - 1:
                acc_ref[here, :] = grad
            else:
                ga_refs[r][...] = grad.astype(row_types[r])
        if r == n_rows - 1:
            total = gb[core]
            if col_acc[step]:
                total += col_sums[step][core][...]
            gb_refs[2 * step + core][...] = total.astype(gb_refs[2 * step + core].dtype)
    for r in range(n_rows):
        la_ref[r] = jnp.sum(loss_ref[pl.ds(r * part, part), :].T, axis=0, keepdims=True)


def tile_terms(rows, cols, row_sums, col_sums, row_types, col_types, diagonal, diag, scales):
    part, width = rows[0].shape
    n_rows, n_pairs = len(rows), len(cols)
    smem = pl.BlockSpec(memory_space=pltpu.SMEM)
    vmem = pl.BlockSpec(memory_space=pltpu.VMEM)
    operands = in_hbm(list(rows) + [v for pair in cols for v in pair])
    operands += [v for v in row_sums if v is not None]
    operands += [v for pair in col_sums if pair is not None for v in pair]
    body = functools.partial(
        tile_kernel,
        [v is not None for v in row_sums],
        [v is not None for v in col_sums],
        row_types,
        diagonal,
    )
    kinds = list(row_types) + [kind for kind in col_types for _ in range(2)]
    out_shape = [
        jax.ShapeDtypeStruct((part, width), F32) if kind == F32 else pltpu.HBM((part, width), kind)
        for kind in kinds
    ]
    n_out = len(out_shape)
    out_shape += [jax.ShapeDtypeStruct((n, 1, part), F32) for n in (n_rows, 2 * n_pairs)]
    out = pl.pallas_call(
        body,
        in_specs=[smem, smem] + [vmem] * len(operands),
        out_specs=[vmem] * len(out_shape),
        out_shape=out_shape,
        scratch_shapes=[
            pltpu.VMEM((n_rows * part if n_pairs > 1 else 8, width), F32),
            pltpu.VMEM((n_rows * part, 128), F32),
        ],
        compiler_params=pltpu.CompilerParams(vmem_limit_bytes=32 * 2**20),
        cost_estimate=pl.CostEstimate(
            flops=6 * n_rows * 2 * n_pairs * part * part * width,
            bytes_accessed=2 * 2 * (n_rows + 2 * n_pairs) * part * width,
            transcendentals=3 * 2 * n_rows * n_pairs * part * part,
        ),
    )(diag, scales, *operands)
    grad_rows, grad_cols = out[:n_rows], out[n_rows:n_out]
    return grad_rows, grad_cols, out[-2].reshape(n_rows, part), out[-1].reshape(n_pairs, 2, part)


def staged(body, smalls, operands, out_shape, cost):
    vmem = pl.BlockSpec(memory_space=pltpu.VMEM)
    return pl.pallas_call(
        body,
        in_specs=[pl.BlockSpec(memory_space=pltpu.SMEM)] * len(smalls) + [vmem] * len(operands),
        out_specs=jax.tree.map(lambda _: vmem, out_shape),
        out_shape=out_shape,
        compiler_params=pltpu.CompilerParams(vmem_limit_bytes=10 * 2**20),
        cost_estimate=pl.CostEstimate(flops=cost, bytes_accessed=2 * cost, transcendentals=0),
    )(*smalls, *in_hbm(operands))


def on_device(features, projection, similarity_scale, logit_bias):
    x, y, c = lax.axis_index("x"), lax.axis_index("y"), lax.axis_index("c")
    m, t = lax.axis_index("m"), lax.axis_index("t")
    inputs = features[0]
    rows, width = inputs.shape
    weight = projection[0]
    half = weight.shape[1]
    part = rows // 2
    pairs = rows * 32
    scale_factor = similarity_scale[0]

    projected = jnp.dot(inputs, weight, preferred_element_type=F32)
    squares = lax.psum(jnp.sum(projected * projected, axis=1), "m")[:, None]
    inverse = lax.rsqrt(squares + 1e-06)
    embedded = (projected * inverse).astype(BF16)
    mine = pick(inputs, c, half, 1)
    others = shifted(pick(inputs, 1 - c, half, 1), "c", 1)

    def rows_for(tower, flip):
        return pick(embedded, jnp.where(t == 0, m ^ flip, 1 ^ tower), part)

    kept = rows_for(0, 0)
    far, near, cross = tied(
        crossed(rows_for(1, 0), 1, 0), crossed(rows_for(0, 1), 0, 1), crossed(rows_for(1, 1), 1, 1)
    )
    own = jnp.concatenate([kept, near], axis=1)
    other = jnp.concatenate([far, cross], axis=1)
    own, other = tied(own, other)

    r1, r3, c1, c3, d0 = tied(
        shifted(own, "y", 1),
        shifted(own, "y", 3),
        shifted(other, "x", 1),
        shifted(other, "x", 3),
        shifted(other, "c", 1),
    )
    c2, r2 = shifted(other, "x", 2), shifted(own, "y", 2)
    d1, d3 = shifted(c1, "c", 1), shifted(c3, "c", 1)
    diag = jnp.where(m == t, 0, 2 * part).astype(jnp.int32).reshape(1)
    scales = jnp.stack([scale_factor, logit_bias[0]]) * math.log2(math.e)
    near = [own, r1, r3]
    cols0, cols1, cols3 = [other, d0], [c1, d1], [c3, d3]
    rows_sum, (a0, b0, a1, b1, a3, b3), la, lb = tile_terms(
        near,
        [cols0, cols1, cols3],
        [None] * 3,
        [None] * 3,
        [F32] * 3,
        [F32] * 3,
        True,
        diag,
        scales,
    )
    c2, r2, a0, b0, a1, b1, a3, b3, *rows_sum = tied(c2, r2, a0, b0, a1, b1, a3, b3, *rows_sum)
    d2 = shifted(c2, "c", 1)
    (sum2,), (s1, t1, s3, t3), la2, lb2 = tile_terms(
        [r2], [cols1, cols3], [None], [[a1, b1], [a3, b3]], [F32], [BF16] * 2, False, diag, scales
    )
    t1, t3 = shifted(t1, "c", 1), shifted(t3, "c", 1)
    (g2,), (s0, t0, a2, b2), la4, lb4 = tile_terms(
        [r2], [cols0, [c2, d2]], [sum2], [[a0, b0], None], [BF16], [BF16, F32], False, diag, scales
    )
    t1, t3, g2, s0, t0, a2, b2 = tied(t1, t3, g2, s0, t0, a2, b2)

    def joined(a, b):
        return (a.astype(F32) + b.astype(F32)).astype(BF16)

    s1, s3, a2, b2 = tied(joined(s1, t1), joined(s3, t3), a2, b2)
    e1, e3 = shifted(s1, "x", 3), shifted(s3, "x", 1)
    f2 = shifted(g2, "y", 2)
    t0 = shifted(t0, "c", 1)
    (g0, g1, g3), (s2, t2), la3, lb3 = tile_terms(
        near, [[c2, d2]], rows_sum, [[a2, b2]], [BF16] * 3, [BF16], False, diag, scales
    )
    loss_rows = jnp.concatenate([la + la3, la2 + la4])
    loss_cols = jnp.stack([lb[0] + lb4[0], lb[1] + lb2[0], lb[2] + lb2[1], lb4[1] + lb3[0]], axis=1)
    e1, e3, f2, t0, g0, g1, g3, s2, t2 = tied(e1, e3, f2, t0, g0, g1, g3, s2, t2)
    s2 = joined(s2, shifted(t2, "c", 1))
    f1, f3 = shifted(g1, "y", 3), shifted(g3, "y", 1)
    e2 = shifted(s2, "x", 2)
    e2, f1, f3 = tied(e2, f1, f3)
    own0, own1 = packed(own, g0, f1, f2, f3)
    other0, other1 = packed(other, s0, t0, e1, e2, e3)
    far, near, cross = tied(crossed(other0, 1, 0), crossed(own1, 0, 1), crossed(other1, 1, 1))
    flags = jnp.stack([t, m]).astype(jnp.int32)
    scale = (scale_factor / pairs).reshape(1)
    grad_proj = unpacked(flags, scale, [own0, far, near, cross], projected, inverse)

    given = shifted(
        jnp.where(c == 0, jnp.stack([loss_rows, loss_rows]), loss_cols), "c", 1
    )
    losses = jnp.where(c == 0, loss_cols + given[::-1], jnp.stack([given[0], loss_rows]))
    losses, grad_proj = tied(losses, grad_proj)
    lines = losses.transpose(1, 0, 2).reshape(4, 1, rows)
    lines = jnp.pad(lines, ((0, 0), (0, 7), (0, half - rows)))

    grad_swap = shifted(grad_proj, "c", 1)
    weight_part = lax.dot_general(
        mine, grad_proj, (((0,), (0,)), ((), ())), preferred_element_type=F32
    ) + lax.dot_general(others, grad_swap, (((0,), (0,)), ((), ())), preferred_element_type=F32)

    small = half // 4
    lead = jnp.where(c == 0, x, y)
    back = jnp.where(c == 0, y, x)

    def message(k):
        block = pick(weight_part, (lead + k) % 4, small)
        return jnp.concatenate([block, lines[{0: 0, 1: 2, 2: 3, 3: 1}[k]]], axis=0)

    a2, a1, a3 = tied(*(turned(message(k), 0, k) for k in STEPS))
    piece = pick(weight_part, lead, small) + a1[:small] + a2[:small] + a3[:small]
    line = (lines[0] + a1[small:] + a2[small:] + a3[small:])[0, :rows].reshape(2, part)
    a2, a1, a3 = tied(*(turned(piece, 1, k) for k in STEPS))
    piece = (piece + a2) + (a1 + a3)
    given = shifted(jnp.where(c == 0, line[1], line[0]), "c", 1)
    loss_rows, loss_cols, piece = tied(
        jnp.where(c == 0, given, line[1]), jnp.where(c == 0, line[0], given), piece
    )
    pieces = [piece] + [turned(piece, 0, k) for k in (1, 3, 2)]
    loss_far = crossed(loss_cols, 1, 0)
    loss_near = crossed(jnp.where(m == 0, loss_rows, loss_far), 0, 1)
    upper = jnp.logical_and(t == 1, m == 1)
    lower = jnp.logical_and(t == 1, m == 0)
    row_loss = (
        jnp.where(lower, 0.0, loss_rows)
        + jnp.where(upper, 0.0, loss_far)
        + jnp.where(t == 1, loss_near, 0.0)
    ) / pairs
    *pieces, row_loss = tied(*pieces, row_loss)
    swapped = [shifted(v, "c", 1) for v in pieces]
    places = [c * half + (lead - k) % 4 * small for k in (0, 1, 3, 2)]
    places += [(1 - c) * half + (back - k) % 4 * small for k in (0, 1, 3, 2)]
    weight_grad = placed_rows(jnp.stack(places).astype(jnp.int32), pieces + swapped)
    return (row_loss[None], weight_grad[None])


def pack_kernel(embed_ref, *refs):
    refs, out_refs = refs[:-2], refs[-2:]
    part, width = embed_ref.shape
    half = width // 2
    total = jnp.zeros((part, 128), F32)
    for k in range(2):
        here = pl.ds(k * half, half)
        grad = sum(ref[:, here].astype(F32) for ref in refs)
        product = grad * embed_ref[:, here].astype(F32)
        total += sum(product[:, i * 128 : (i + 1) * 128] for i in range(half // 128))
        out_refs[k][:part, :] = grad.astype(BF16)
    line = jnp.sum(total.T, axis=0, keepdims=True)
    parts = []
    for _ in range(3):
        parts.append(line.astype(BF16).astype(F32))
        line = line - parts[-1]
    extra = jnp.broadcast_to(jnp.concatenate(parts, axis=1), (EXTRA, 3 * part)).astype(BF16)
    for k in range(2):
        out_refs[k][part:, :] = extra


def packed(embed, *grads):
    part, width = embed.shape
    out = [pltpu.HBM((part + EXTRA, width // 2), BF16)] * 2
    return staged(pack_kernel, (), (embed,) + grads, out, 6 * part * width)


def unpack_kernel(flags_ref, scale_ref, p00, p10, p01, p11, projected_ref, inverse_ref, out_ref):
    part = p00.shape[0] - EXTRA
    t, m = flags_ref[0], flags_ref[1]
    scale = scale_ref[0]

    def finish(first, second, here):
        grad = first[:part, :].astype(F32) + second[:part, :].astype(F32)
        line = first[part : part + 1, :].astype(F32) + second[part : part + 1, :].astype(F32)
        line = line[:, :part] + line[:, part : 2 * part] + line[:, 2 * part :]
        along = jnp.broadcast_to(line, (128, part)).T[:, :1]
        inverse = inverse_ref[here, :]
        result = inverse * scale * (grad - inverse * along * projected_ref[here, :])
        out_ref[here, :] = result.astype(BF16)

    low, high = pl.ds(0, part), pl.ds(part, part)

    @pl.when(jnp.logical_and(t == 0, m == 0))
    def _():
        finish(p00, p10, low)
        finish(p01, p11, high)

    @pl.when(jnp.logical_and(t == 0, m == 1))
    def _():
        finish(p01, p11, low)
        finish(p00, p10, high)

    @pl.when(t == 1)
    def _():
        finish(p10, p11, low)
        finish(p00, p01, high)


def unpacked(flags, scale, pieces, projected, inverse):
    out = jax.ShapeDtypeStruct(projected.shape, BF16)
    operands = (*pieces, projected, inverse)
    return staged(unpack_kernel, (flags, scale), operands, out, 6 * projected.size)


def turned(value, late, step):
    route = []
    for i in range(32):
        x, y, c = i // 8, i // 2 % 4, i % 2
        if c ^ late:
            y = (y + step) % 4
        else:
            x = (x + step) % 4
        route.append((i, x * 8 + y * 2 + c))
    return lax.ppermute(value, ("x", "y", "c"), route)


def place_kernel(places_ref, *refs):
    *pieces, out_ref, sems = refs
    copies = []
    for i, piece in enumerate(pieces):
        size = piece.shape[0]
        here = pl.ds(pl.multiple_of(places_ref[i], size), size)
        copies.append(pltpu.make_async_copy(piece, out_ref.at[here, :], sems.at[i]))
        copies[-1].start()
    for copy in copies:
        copy.wait()


def placed_rows(places, pieces):
    size, width = pieces[0].shape
    count = len(pieces)
    return pl.pallas_call(
        place_kernel,
        in_specs=[pl.BlockSpec(memory_space=pltpu.SMEM)]
        + [pl.BlockSpec(memory_space=pltpu.VMEM)] * count,
        out_specs=pl.BlockSpec(memory_space=pltpu.HBM),
        out_shape=pltpu.HBM((size * count, width), F32),
        scratch_shapes=[pltpu.SemaphoreType.DMA((count,))],
        compiler_params=pltpu.CompilerParams(vmem_limit_bytes=10 * 2**20),
    )(places, *in_hbm(pieces))


def solution(mesh):
    fine = Mesh(mesh.devices.reshape(4, 4, 2, 2, 2), ("x", "y", "c", "m", "t"))
    dp = ("x", "y", "c")
    placed = (P("t", dp, None), P("t", None, "m"), P(), P())
    return jax.shard_map(
        on_device,
        mesh=fine,
        in_specs=placed,
        out_specs=(P("t", dp + ("m",)), P("t", None, "m")),
        check_vma=False,
    )
```

```python
import functools
import math

import jax
import jax.numpy as jnp
from jax import lax
from jax.experimental import pallas as pl
from jax.experimental.pallas import tpu as pltpu
from jax.sharding import Mesh, PartitionSpec as P

F32 = jnp.float32
BF16 = jnp.bfloat16
STEPS = (2, 1, 3)
EXTRA = 16
LINES = (0, 2, 3, 1)


def shifted(value, axis, step):
    count = lax.axis_size(axis)
    return lax.ppermute(value, axis, [(i, (i + step) % count) for i in range(count)])


def crossed(value, tower, half):
    flip = 2 * half + tower
    return lax.ppermute(value, ("m", "t"), [(i, i ^ flip) for i in range(4)])


def pick(block, index, size, axis=0):
    return lax.dynamic_slice_in_dim(block, index * size, size, axis)


def tied(*values):
    return lax.optimization_barrier(values)


def in_hbm(values):
    return [pltpu.with_memory_space_constraint(v, pltpu.HBM) for v in values]


def tile_kernel(row_acc, col_acc, row_types, diagonal, *refs):
    refs = list(refs)
    n_rows, n_pairs = len(row_acc), len(col_acc)

    def take(count):
        return [refs.pop(0) for _ in range(count)]

    diag_ref, scale_ref = take(2)
    rows_refs = take(n_rows)
    cols_refs = [take(2) for _ in range(n_pairs)]
    row_sums = [refs.pop(0) if has else None for has in row_acc]
    col_sums = [take(2) if has else None for has in col_acc]
    ga_refs, gb_refs = take(n_rows), take(2 * n_pairs)
    la_ref, lb_ref, acc_ref, loss_ref = take(4)
    part, width = rows_refs[0].shape
    scale = scale_ref[0]
    bias = scale_ref[1]

    def products(step, r, core):
        return lax.dot_general(
            rows_refs[r][...],
            cols_refs[step][core][...],
            (((1,), (1,)), ((), ())),
            preferred_element_type=F32,
        )

    order = [(k, r, core) for k in range(n_pairs) for r in range(n_rows) for core in range(2)]
    coming = products(*order[0])
    for i, (step, r, core) in enumerate(order):
        logits = coming * scale + bias
        if i + 1 < len(order):
            coming = products(*order[i + 1])
        here = pl.ds(r * part, part)
        if r == 0 and core == 0:
            gb = [jnp.zeros((part, width), F32) for _ in range(2)]
        if core == 0:
            grad = jnp.zeros((part, width), F32)
        meets = diagonal and i == 0
        if meets:
            image = lax.broadcasted_iota(jnp.int32, (part, part), 0)
            text = lax.broadcasted_iota(jnp.int32, (part, part), 1)
            same = image + diag_ref[0] == text
            logits = jnp.where(same, -logits, logits)
        grown = jnp.exp2(logits)
        whole = 1.0 + grown
        inverse = pl.reciprocal(whole, approx=True)
        inverse = inverse * (2.0 - whole * inverse)
        losses = jnp.log(whole) + (grown - (whole - 1.0)) * inverse
        share = grown * inverse
        if meets:
            share = jnp.where(same, -share, share)
        coefficient = share.astype(BF16)
        folded = sum(losses[:, k * 128 : (k + 1) * 128] for k in range(part // 128))
        column = jnp.sum(losses, axis=0, keepdims=True)
        if step == 0 and core == 0:
            loss_ref[here, :] = folded
        else:
            loss_ref[here, :] += folded
        if r == 0:
            lb_ref[2 * step + core] = column
        else:
            lb_ref[2 * step + core] += column
        grad += jnp.dot(coefficient, cols_refs[step][core][...], preferred_element_type=F32)
        gb[core] += lax.dot_general(
            coefficient, rows_refs[r][...], (((0,), (0,)), ((), ())), preferred_element_type=F32
        )
        if core == 1:
            if step == 0 and row_acc[r]:
                grad += row_sums[r][...]
            if step > 0:
                grad += acc_ref[here, :]
            if step < n_pairs - 1:
                acc_ref[here, :] = grad
            else:
                ga_refs[r][...] = grad.astype(row_types[r])
        if r == n_rows - 1:
            total = gb[core]
            if col_acc[step]:
                total += col_sums[step][core][...]
            gb_refs[2 * step + core][...] = total.astype(gb_refs[2 * step + core].dtype)
    for r in range(n_rows):
        la_ref[r] = jnp.sum(loss_ref[pl.ds(r * part, part), :].T, axis=0, keepdims=True)


def tile_terms(rows, cols, row_sums, col_sums, row_types, col_types, diagonal, diag, scales):
    part, width = rows[0].shape
    n_rows, n_pairs = len(rows), len(cols)
    smem = pl.BlockSpec(memory_space=pltpu.SMEM)
    vmem = pl.BlockSpec(memory_space=pltpu.VMEM)
    operands = in_hbm(list(rows) + [v for pair in cols for v in pair])
    operands += [v for v in row_sums if v is not None]
    operands += [v for pair in col_sums if pair is not None for v in pair]
    body = functools.partial(
        tile_kernel,
        [v is not None for v in row_sums],
        [v is not None for v in col_sums],
        row_types,
        diagonal,
    )
    kinds = list(row_types) + [kind for kind in col_types for _ in range(2)]
    out_shape = [
        jax.ShapeDtypeStruct((part, width), F32) if kind == F32 else pltpu.HBM((part, width), kind)
        for kind in kinds
    ]
    n_out = len(out_shape)
    out_shape += [jax.ShapeDtypeStruct((n, 1, part), F32) for n in (n_rows, 2 * n_pairs)]
    out = pl.pallas_call(
        body,
        in_specs=[smem, smem] + [vmem] * len(operands),
        out_specs=[vmem] * len(out_shape),
        out_shape=out_shape,
        scratch_shapes=[
            pltpu.VMEM((n_rows * part if n_pairs > 1 else 8, width), F32),
            pltpu.VMEM((n_rows * part, 128), F32),
        ],
        compiler_params=pltpu.CompilerParams(vmem_limit_bytes=32 * 2**20),
        cost_estimate=pl.CostEstimate(
            flops=6 * n_rows * 2 * n_pairs * part * part * width,
            bytes_accessed=2 * 2 * (n_rows + 2 * n_pairs) * part * width,
            transcendentals=3 * 2 * n_rows * n_pairs * part * part,
        ),
    )(diag, scales, *operands)
    grad_rows, grad_cols = out[:n_rows], out[n_rows:n_out]
    return grad_rows, grad_cols, out[-2].reshape(n_rows, part), out[-1].reshape(n_pairs, 2, part)


def staged(body, smalls, operands, out_shape, cost):
    vmem = pl.BlockSpec(memory_space=pltpu.VMEM)
    return pl.pallas_call(
        body,
        in_specs=[pl.BlockSpec(memory_space=pltpu.SMEM)] * len(smalls) + [vmem] * len(operands),
        out_specs=jax.tree.map(lambda _: vmem, out_shape),
        out_shape=out_shape,
        compiler_params=pltpu.CompilerParams(vmem_limit_bytes=10 * 2**20),
        cost_estimate=pl.CostEstimate(flops=cost, bytes_accessed=2 * cost, transcendentals=0),
    )(*smalls, *in_hbm(operands))


def on_device(features, projection, similarity_scale, logit_bias):
    x, y, c = lax.axis_index("x"), lax.axis_index("y"), lax.axis_index("c")
    m, t = lax.axis_index("m"), lax.axis_index("t")
    inputs = features[0]
    rows, width = inputs.shape
    weight = projection[0]
    half = weight.shape[1]
    part = rows // 2
    pairs = rows * 32
    scale_factor = similarity_scale[0]

    projected = jnp.dot(inputs, weight, preferred_element_type=F32)
    squares = lax.psum(jnp.sum(projected * projected, axis=1), "m")[:, None]
    inverse = lax.rsqrt(squares + 1e-06)
    embedded = (projected * inverse).astype(BF16)
    mine = pick(inputs, c, half, 1)
    others = shifted(pick(inputs, 1 - c, half, 1), "c", 1)

    def rows_for(tower, flip):
        return pick(embedded, jnp.where(t == 0, m ^ flip, 1 ^ tower), part)

    kept = rows_for(0, 0)
    far, near, cross = tied(
        crossed(rows_for(1, 0), 1, 0), crossed(rows_for(0, 1), 0, 1), crossed(rows_for(1, 1), 1, 1)
    )
    own = jnp.concatenate([kept, near], axis=1)
    other = jnp.concatenate([far, cross], axis=1)
    own, other = tied(own, other)

    r1, r3, c1, c3, d0 = tied(
        shifted(own, "y", 1),
        shifted(own, "y", 3),
        shifted(other, "x", 1),
        shifted(other, "x", 3),
        shifted(other, "c", 1),
    )
    c2, r2 = shifted(other, "x", 2), shifted(own, "y", 2)
    d1, d3 = shifted(c1, "c", 1), shifted(c3, "c", 1)
    diag = jnp.where(m == t, 0, 2 * part).astype(jnp.int32).reshape(1)
    scales = jnp.stack([scale_factor, logit_bias[0]]) * math.log2(math.e)
    near = [own, r1, r3]
    cols0, cols1, cols3 = [other, d0], [c1, d1], [c3, d3]
    rows_sum, (a0, b0, a1, b1, a3, b3), la, lb = tile_terms(
        near,
        [cols0, cols1, cols3],
        [None] * 3,
        [None] * 3,
        [F32] * 3,
        [F32] * 3,
        True,
        diag,
        scales,
    )
    c2, r2, a0, b0, a1, b1, a3, b3, *rows_sum = tied(c2, r2, a0, b0, a1, b1, a3, b3, *rows_sum)
    d2 = shifted(c2, "c", 1)
    (sum2,), (s1, t1, s3, t3), la2, lb2 = tile_terms(
        [r2], [cols1, cols3], [None], [[a1, b1], [a3, b3]], [F32], [BF16] * 2, False, diag, scales
    )
    t1, t3 = shifted(t1, "c", 1), shifted(t3, "c", 1)
    (g2,), (s0, t0, a2, b2), la4, lb4 = tile_terms(
        [r2], [cols0, [c2, d2]], [sum2], [[a0, b0], None], [BF16], [BF16, F32], False, diag, scales
    )
    t1, t3, g2, s0, t0, a2, b2 = tied(t1, t3, g2, s0, t0, a2, b2)

    def joined(a, b):
        return (a.astype(F32) + b.astype(F32)).astype(BF16)

    s1, s3, a2, b2 = tied(joined(s1, t1), joined(s3, t3), a2, b2)
    e1, e3 = shifted(s1, "x", 3), shifted(s3, "x", 1)
    f2 = shifted(g2, "y", 2)
    t0 = shifted(t0, "c", 1)
    (g0, g1, g3), (s2, t2), la3, lb3 = tile_terms(
        near, [[c2, d2]], rows_sum, [[a2, b2]], [BF16] * 3, [BF16], False, diag, scales
    )
    loss_rows = jnp.concatenate([la + la3, la2 + la4])
    loss_cols = jnp.stack([lb[0] + lb4[0], lb[1] + lb2[0], lb[2] + lb2[1], lb4[1] + lb3[0]], axis=1)
    e1, e3, f2, t0, g0, g1, g3, s2, t2 = tied(e1, e3, f2, t0, g0, g1, g3, s2, t2)
    s2 = joined(s2, shifted(t2, "c", 1))
    f1, f3 = shifted(g1, "y", 3), shifted(g3, "y", 1)
    e2 = shifted(s2, "x", 2)
    e2, f1, f3 = tied(e2, f1, f3)
    own0, own1 = packed(own, g0, f1, f2, f3)
    other0, other1 = packed(other, s0, t0, e1, e2, e3)
    far, near, cross = tied(crossed(other0, 1, 0), crossed(own1, 0, 1), crossed(other1, 1, 1))
    flags = jnp.stack([t, m]).astype(jnp.int32)
    scale = (scale_factor / pairs).reshape(1)
    grad_proj = unpacked(flags, scale, [own0, far, near, cross], projected, inverse)

    given = shifted(
        jnp.where(c == 0, jnp.stack([loss_rows, loss_rows]), loss_cols), "c", 1
    )
    losses = jnp.where(c == 0, loss_cols + given[::-1], jnp.stack([given[0], loss_rows]))
    losses, grad_proj = tied(losses, grad_proj)
    lines = losses.transpose(1, 0, 2).reshape(4, 1, rows)
    lines = jnp.pad(lines, ((0, 0), (0, 7), (0, half - rows)))

    grad_swap = shifted(grad_proj, "c", 1)
    small = half // 4
    lead = jnp.where(c == 0, x, y)
    back = jnp.where(c == 0, y, x)
    keep, m1, m2, m3 = weight_messages(
        lead.reshape(1).astype(jnp.int32), mine, others, grad_proj, grad_swap, lines
    )
    a2, a1, a3 = tied(turned(m2, 0, 2), turned(m1, 0, 1), turned(m3, 0, 3))
    total = keep + a1 + a2 + a3
    piece = total[:small]
    line = total[small, :rows].reshape(2, part)
    a2, a1, a3 = tied(*(turned(piece, 1, k) for k in STEPS))
    piece = (piece + a2) + (a1 + a3)
    given = shifted(jnp.where(c == 0, line[1], line[0]), "c", 1)
    loss_rows, loss_cols = jnp.where(c == 0, given, line[1]), jnp.where(c == 0, line[0], given)
    loss_far = crossed(loss_cols, 1, 0)
    loss_near = crossed(jnp.where(m == 0, loss_rows, loss_far), 0, 1)
    upper = jnp.logical_and(t == 1, m == 1)
    lower = jnp.logical_and(t == 1, m == 0)
    row_loss = (
        jnp.where(lower, 0.0, loss_rows)
        + jnp.where(upper, 0.0, loss_far)
        + jnp.where(t == 1, loss_near, 0.0)
    ) / pairs
    row_loss, piece = tied(row_loss, piece)
    p2, p1, p3, first = tied(*(turned(piece, 0, k) for k in STEPS), shifted(piece, "c", 1))
    pieces = [piece, p1, p3, p2]
    swapped = [shifted(v, "c", 1) for v in pieces[1:]]
    places = [c * half + (lead - k) % 4 * small for k in (0, 1, 3, 2)]
    others = [(1 - c) * half + (back - k) % 4 * small for k in (0, 1, 3, 2)]
    weight_grad = placed_rows(places + others[:1], pieces + [first], None)
    *swapped, weight_grad = tied(*swapped, weight_grad)
    weight_grad = placed_rows(others[1:], swapped, weight_grad)
    return (row_loss[None], weight_grad[None])


def pack_kernel(embed_ref, *refs):
    refs, out_refs = refs[:-2], refs[-2:]
    part, width = embed_ref.shape
    half = width // 2
    total = jnp.zeros((part, 128), F32)
    for k in range(2):
        here = pl.ds(k * half, half)
        grad = sum(ref[:, here].astype(F32) for ref in refs)
        product = grad * embed_ref[:, here].astype(F32)
        total += sum(product[:, i * 128 : (i + 1) * 128] for i in range(half // 128))
        out_refs[k][:part, :] = grad.astype(BF16)
    line = jnp.sum(total.T, axis=0, keepdims=True)
    parts = []
    for _ in range(3):
        parts.append(line.astype(BF16).astype(F32))
        line = line - parts[-1]
    extra = jnp.broadcast_to(jnp.concatenate(parts, axis=1), (EXTRA, 3 * part)).astype(BF16)
    for k in range(2):
        out_refs[k][part:, :] = extra


def packed(embed, *grads):
    part, width = embed.shape
    out = [pltpu.HBM((part + EXTRA, width // 2), BF16)] * 2
    return staged(pack_kernel, (), (embed,) + grads, out, 6 * part * width)


def unpack_kernel(flags_ref, scale_ref, p00, p10, p01, p11, projected_ref, inverse_ref, out_ref):
    part = p00.shape[0] - EXTRA
    t, m = flags_ref[0], flags_ref[1]
    scale = scale_ref[0]

    def finish(first, second, here):
        grad = first[:part, :].astype(F32) + second[:part, :].astype(F32)
        line = first[part : part + 1, :].astype(F32) + second[part : part + 1, :].astype(F32)
        line = line[:, :part] + line[:, part : 2 * part] + line[:, 2 * part :]
        along = jnp.broadcast_to(line, (128, part)).T[:, :1]
        inverse = inverse_ref[here, :]
        result = inverse * scale * (grad - inverse * along * projected_ref[here, :])
        out_ref[here, :] = result.astype(BF16)

    low, high = pl.ds(0, part), pl.ds(part, part)

    @pl.when(jnp.logical_and(t == 0, m == 0))
    def _():
        finish(p00, p10, low)
        finish(p01, p11, high)

    @pl.when(jnp.logical_and(t == 0, m == 1))
    def _():
        finish(p01, p11, low)
        finish(p00, p10, high)

    @pl.when(t == 1)
    def _():
        finish(p10, p11, low)
        finish(p00, p01, high)


def unpacked(flags, scale, pieces, projected, inverse):
    out = jax.ShapeDtypeStruct(projected.shape, BF16)
    operands = (*pieces, projected, inverse)
    return staged(unpack_kernel, (flags, scale), operands, out, 6 * projected.size)


def turned(value, late, step):
    route = []
    for i in range(32):
        x, y, c = i // 8, i // 2 % 4, i % 2
        if c ^ late:
            y = (y + step) % 4
        else:
            x = (x + step) % 4
        route.append((i, x * 8 + y * 2 + c))
    return lax.ppermute(value, ("x", "y", "c"), route)


def weight_kernel(lead_ref, mine, others, own_grad, other_grad, lines, *refs):
    *outs, total_ref = refs
    small = outs[0].shape[0] - lines.shape[1]
    total_ref[...] = lax.dot_general(
        mine[...], own_grad[...], (((0,), (0,)), ((), ())), preferred_element_type=F32
    ) + lax.dot_general(
        others[...], other_grad[...], (((0,), (0,)), ((), ())), preferred_element_type=F32
    )
    for k, out in enumerate(outs):
        here = pl.multiple_of((lead_ref[0] + k) % 4 * small, small)
        out[:small, :] = total_ref[pl.ds(here, small), :]
        out[small:, :] = lines[LINES[k]]


def weight_messages(lead, mine, others, own_grad, other_grad, lines):
    half = mine.shape[1]
    small = half // 4
    vmem = pl.BlockSpec(memory_space=pltpu.VMEM)
    message = jax.ShapeDtypeStruct((small + lines.shape[1], half), F32)
    return pl.pallas_call(
        weight_kernel,
        in_specs=[pl.BlockSpec(memory_space=pltpu.SMEM)] + [vmem] * 5,
        out_specs=[vmem] * 4,
        out_shape=[message] * 4,
        scratch_shapes=[pltpu.VMEM((half, half), F32)],
        compiler_params=pltpu.CompilerParams(vmem_limit_bytes=14 * 2**20),
        cost_estimate=pl.CostEstimate(
            flops=4 * mine.size * half, bytes_accessed=8 * mine.size, transcendentals=0
        ),
    )(lead, mine, others, own_grad, other_grad, lines)


def place_kernel(count, places_ref, *refs):
    pieces, out_ref, sems = refs[:count], refs[-2], refs[-1]
    copies = []
    for i, piece in enumerate(pieces):
        size = piece.shape[0]
        here = pl.ds(pl.multiple_of(places_ref[i], size), size)
        copies.append(pltpu.make_async_copy(piece, out_ref.at[here, :], sems.at[i]))
        copies[-1].start()
    for copy in copies:
        copy.wait()


def placed_rows(places, pieces, target):
    size, width = pieces[0].shape
    count = len(pieces)
    operands = in_hbm(pieces)
    specs = [pl.BlockSpec(memory_space=pltpu.VMEM)] * count
    if target is not None:
        operands += in_hbm([target])
        specs += [pl.BlockSpec(memory_space=pltpu.HBM)]
    return pl.pallas_call(
        functools.partial(place_kernel, count),
        in_specs=[pl.BlockSpec(memory_space=pltpu.SMEM)] + specs,
        out_specs=pl.BlockSpec(memory_space=pltpu.HBM),
        out_shape=pltpu.HBM((8 * size, width), F32),
        scratch_shapes=[pltpu.SemaphoreType.DMA((count,))],
        input_output_aliases={} if target is None else {count + 1: 0},
        compiler_params=pltpu.CompilerParams(vmem_limit_bytes=10 * 2**20),
    )(jnp.stack(places).astype(jnp.int32), *operands)


def solution(mesh):
    fine = Mesh(mesh.devices.reshape(4, 4, 2, 2, 2), ("x", "y", "c", "m", "t"))
    dp = ("x", "y", "c")
    placed = (P("t", dp, None), P("t", None, "m"), P(), P())
    return jax.shard_map(
        on_device,
        mesh=fine,
        in_specs=placed,
        out_specs=(P("t", dp + ("m",)), P("t", None, "m")),
        check_vma=False,
    )
```

```python
import functools
import math

import jax
import jax.numpy as jnp
from jax import lax
from jax.experimental import pallas as pl
from jax.experimental.pallas import tpu as pltpu
from jax.sharding import Mesh, PartitionSpec as P

F32 = jnp.float32
BF16 = jnp.bfloat16
STEPS = (2, 1, 3)
EXTRA = 16
LINES = (0, 2, 3, 1)


def shifted(value, axis, step):
    count = lax.axis_size(axis)
    return lax.ppermute(value, axis, [(i, (i + step) % count) for i in range(count)])


def crossed(value, tower, half):
    flip = 2 * half + tower
    return lax.ppermute(value, ("m", "t"), [(i, i ^ flip) for i in range(4)])


def pick(block, index, size, axis=0):
    return lax.dynamic_slice_in_dim(block, index * size, size, axis)


def tied(*values):
    return lax.optimization_barrier(values)


def in_hbm(values):
    return [pltpu.with_memory_space_constraint(v, pltpu.HBM) for v in values]


def tile_kernel(row_acc, col_acc, row_types, diagonal, *refs):
    refs = list(refs)
    n_rows, n_pairs = len(row_acc), len(col_acc)

    def take(count):
        return [refs.pop(0) for _ in range(count)]

    diag_ref, scale_ref = take(2)
    rows_refs = take(n_rows)
    cols_refs = [take(2) for _ in range(n_pairs)]
    row_sums = [refs.pop(0) if has else None for has in row_acc]
    col_sums = [take(2) if has else None for has in col_acc]
    ga_refs, gb_refs = take(n_rows), take(2 * n_pairs)
    la_ref, lb_ref, acc_ref, loss_ref = take(4)
    part, width = rows_refs[0].shape
    scale = scale_ref[0]
    bias = scale_ref[1]

    def products(step, r, core):
        return lax.dot_general(
            rows_refs[r][...],
            cols_refs[step][core][...],
            (((1,), (1,)), ((), ())),
            preferred_element_type=F32,
        )

    order = [(k, r, core) for k in range(n_pairs) for r in range(n_rows) for core in range(2)]
    coming = products(*order[0])
    for i, (step, r, core) in enumerate(order):
        logits = coming * scale + bias
        if i + 1 < len(order):
            coming = products(*order[i + 1])
        here = pl.ds(r * part, part)
        if r == 0 and core == 0:
            gb = [jnp.zeros((part, width), F32) for _ in range(2)]
        if core == 0:
            grad = jnp.zeros((part, width), F32)
        meets = diagonal and i == 0
        if meets:
            image = lax.broadcasted_iota(jnp.int32, (part, part), 0)
            text = lax.broadcasted_iota(jnp.int32, (part, part), 1)
            same = image + diag_ref[0] == text
            logits = jnp.where(same, -logits, logits)
        grown = jnp.exp2(logits)
        whole = 1.0 + grown
        inverse = pl.reciprocal(whole, approx=True)
        inverse = inverse * (2.0 - whole * inverse)
        losses = jnp.log(whole) + (grown - (whole - 1.0)) * inverse
        share = grown * inverse
        if meets:
            share = jnp.where(same, -share, share)
        coefficient = share.astype(BF16)
        folded = sum(losses[:, k * 128 : (k + 1) * 128] for k in range(part // 128))
        column = jnp.sum(losses, axis=0, keepdims=True)
        if step == 0 and core == 0:
            loss_ref[here, :] = folded
        else:
            loss_ref[here, :] += folded
        if r == 0:
            lb_ref[2 * step + core] = column
        else:
            lb_ref[2 * step + core] += column
        grad += jnp.dot(coefficient, cols_refs[step][core][...], preferred_element_type=F32)
        gb[core] += lax.dot_general(
            coefficient, rows_refs[r][...], (((0,), (0,)), ((), ())), preferred_element_type=F32
        )
        if core == 1:
            if step == 0 and row_acc[r]:
                grad += row_sums[r][...]
            if step > 0:
                grad += acc_ref[here, :]
            if step < n_pairs - 1:
                acc_ref[here, :] = grad
            else:
                ga_refs[r][...] = grad.astype(row_types[r])
        if r == n_rows - 1:
            total = gb[core]
            if col_acc[step]:
                total += col_sums[step][core][...]
            gb_refs[2 * step + core][...] = total.astype(gb_refs[2 * step + core].dtype)
    for r in range(n_rows):
        la_ref[r] = jnp.sum(loss_ref[pl.ds(r * part, part), :].T, axis=0, keepdims=True)


def tile_terms(rows, cols, row_sums, col_sums, row_types, col_types, diagonal, diag, scales, far=()):
    part, width = rows[0].shape
    n_rows, n_pairs = len(rows), len(cols)
    smem = pl.BlockSpec(memory_space=pltpu.SMEM)
    vmem = pl.BlockSpec(memory_space=pltpu.VMEM)
    operands = list(rows) + [v for pair in cols for v in pair]
    held = set(map(id, far))
    operands = [v if id(v) in held else in_hbm([v])[0] for v in operands]
    operands += [v for v in row_sums if v is not None]
    operands += [v for pair in col_sums if pair is not None for v in pair]
    body = functools.partial(
        tile_kernel,
        [v is not None for v in row_sums],
        [v is not None for v in col_sums],
        row_types,
        diagonal,
    )
    kinds = list(row_types) + [kind for kind in col_types for _ in range(2)]
    out_shape = [
        jax.ShapeDtypeStruct((part, width), F32) if kind == F32 else pltpu.HBM((part, width), kind)
        for kind in kinds
    ]
    n_out = len(out_shape)
    out_shape += [jax.ShapeDtypeStruct((n, 1, part), F32) for n in (n_rows, 2 * n_pairs)]
    out = pl.pallas_call(
        body,
        in_specs=[smem, smem] + [vmem] * len(operands),
        out_specs=[vmem] * len(out_shape),
        out_shape=out_shape,
        scratch_shapes=[
            pltpu.VMEM((n_rows * part if n_pairs > 1 else 8, width), F32),
            pltpu.VMEM((n_rows * part, 128), F32),
        ],
        compiler_params=pltpu.CompilerParams(vmem_limit_bytes=32 * 2**20),
        cost_estimate=pl.CostEstimate(
            flops=6 * n_rows * 2 * n_pairs * part * part * width,
            bytes_accessed=2 * 2 * (n_rows + 2 * n_pairs) * part * width,
            transcendentals=3 * 2 * n_rows * n_pairs * part * part,
        ),
    )(diag, scales, *operands)
    grad_rows, grad_cols = out[:n_rows], out[n_rows:n_out]
    return grad_rows, grad_cols, out[-2].reshape(n_rows, part), out[-1].reshape(n_pairs, 2, part)


def staged(body, smalls, operands, out_shape, cost, held=False):
    vmem = pl.BlockSpec(memory_space=pltpu.VMEM)
    return pl.pallas_call(
        body,
        in_specs=[pl.BlockSpec(memory_space=pltpu.SMEM)] * len(smalls) + [vmem] * len(operands),
        out_specs=jax.tree.map(lambda _: vmem, out_shape),
        out_shape=out_shape,
        compiler_params=pltpu.CompilerParams(vmem_limit_bytes=10 * 2**20),
        cost_estimate=pl.CostEstimate(flops=cost, bytes_accessed=2 * cost, transcendentals=0),
    )(*smalls, *(in_hbm(operands) if held else operands))


def on_device(features, projection, similarity_scale, logit_bias):
    x, y, c = lax.axis_index("x"), lax.axis_index("y"), lax.axis_index("c")
    m, t = lax.axis_index("m"), lax.axis_index("t")
    inputs = features[0]
    rows, width = inputs.shape
    weight = projection[0]
    half = weight.shape[1]
    part = rows // 2
    pairs = rows * 32
    scale_factor = similarity_scale[0]

    projected = jnp.dot(inputs, weight, preferred_element_type=F32)
    squares = lax.psum(jnp.sum(projected * projected, axis=1), "m")[:, None]
    inverse = lax.rsqrt(squares + 1e-06)
    embedded = (projected * inverse).astype(BF16)
    mine = pick(inputs, c, half, 1)
    others = shifted(pick(inputs, 1 - c, half, 1), "c", 1)

    def rows_for(tower, flip):
        return pick(embedded, jnp.where(t == 0, m ^ flip, 1 ^ tower), part)

    kept = rows_for(0, 0)
    far, near, cross = tied(
        crossed(rows_for(1, 0), 1, 0), crossed(rows_for(0, 1), 0, 1), crossed(rows_for(1, 1), 1, 1)
    )
    own = jnp.concatenate([kept, near], axis=1)
    other = jnp.concatenate([far, cross], axis=1)
    own, other = tied(own, other)

    r1, r3, c1, c3, d0 = tied(
        shifted(own, "y", 1),
        shifted(own, "y", 3),
        shifted(other, "x", 1),
        shifted(other, "x", 3),
        shifted(other, "c", 1),
    )
    c2, r2 = shifted(other, "x", 2), shifted(own, "y", 2)
    d1, d3 = shifted(c1, "c", 1), shifted(c3, "c", 1)
    diag = jnp.where(m == t, 0, 2 * part).astype(jnp.int32).reshape(1)
    scales = jnp.stack([scale_factor, logit_bias[0]]) * math.log2(math.e)
    near = [own, r1, r3]
    cols0, cols1, cols3 = [other, d0], [c1, d1], [c3, d3]
    rows_sum, (a0, b0, a1, b1, a3, b3), la, lb = tile_terms(
        near,
        [cols0, cols1, cols3],
        [None] * 3,
        [None] * 3,
        [F32] * 3,
        [F32] * 3,
        True,
        diag,
        scales,
    )
    c2, r2, a0, b0, a1, b1, a3, b3, *rows_sum = tied(c2, r2, a0, b0, a1, b1, a3, b3, *rows_sum)
    d2 = shifted(c2, "c", 1)
    (sum2,), (s1, t1, s3, t3), la2, lb2 = tile_terms(
        [r2],
        [cols1, cols3],
        [None],
        [[a1, b1], [a3, b3]],
        [F32],
        [BF16] * 2,
        False,
        diag,
        scales,
        [r2],
    )
    t1, t3 = shifted(t1, "c", 1), shifted(t3, "c", 1)
    (g2,), (s0, t0, a2, b2), la4, lb4 = tile_terms(
        [r2],
        [cols0, [c2, d2]],
        [sum2],
        [[a0, b0], None],
        [BF16],
        [BF16, F32],
        False,
        diag,
        scales,
        [r2, c2, d2],
    )
    t1, t3, g2, s0, t0, a2, b2 = tied(t1, t3, g2, s0, t0, a2, b2)

    def joined(a, b):
        return (a.astype(F32) + b.astype(F32)).astype(BF16)

    s1, s3, a2, b2 = tied(joined(s1, t1), joined(s3, t3), a2, b2)
    e1, e3 = shifted(s1, "x", 3), shifted(s3, "x", 1)
    f2 = shifted(g2, "y", 2)
    t0 = shifted(t0, "c", 1)
    (g0, g1, g3), (s2, t2), la3, lb3 = tile_terms(
        near,
        [[c2, d2]],
        rows_sum,
        [[a2, b2]],
        [BF16] * 3,
        [BF16],
        False,
        diag,
        scales,
        [c2, d2],
    )
    loss_rows = jnp.concatenate([la + la3, la2 + la4])
    loss_cols = jnp.stack([lb[0] + lb4[0], lb[1] + lb2[0], lb[2] + lb2[1], lb4[1] + lb3[0]], axis=1)
    e1, e3, f2, t0, g0, g1, g3, s2, t2 = tied(e1, e3, f2, t0, g0, g1, g3, s2, t2)
    s2 = joined(s2, shifted(t2, "c", 1))
    f1, f3 = shifted(g1, "y", 3), shifted(g3, "y", 1)
    e2 = shifted(s2, "x", 2)
    e2, f1, f3 = tied(e2, f1, f3)
    own0, own1 = packed(own, g0, f1, f2, f3)
    other0, other1 = packed(other, s0, t0, e1, e2, e3)
    far, near, cross = tied(crossed(other0, 1, 0), crossed(own1, 0, 1), crossed(other1, 1, 1))
    flags = jnp.stack([t, m]).astype(jnp.int32)
    scale = (scale_factor / pairs).reshape(1)
    grad_proj = unpacked(flags, scale, [own0, far, near, cross], projected, inverse)

    given = shifted(
        jnp.where(c == 0, jnp.stack([loss_rows, loss_rows]), loss_cols), "c", 1
    )
    losses = jnp.where(c == 0, loss_cols + given[::-1], jnp.stack([given[0], loss_rows]))
    losses, grad_proj = tied(losses, grad_proj)
    lines = losses.transpose(1, 0, 2).reshape(4, 1, rows)
    lines = jnp.pad(lines, ((0, 0), (0, 7), (0, half - rows)))

    grad_swap = shifted(grad_proj, "c", 1)
    small = half // 4
    lead = jnp.where(c == 0, x, y)
    back = jnp.where(c == 0, y, x)
    keep, m1, m2, m3 = weight_messages(
        lead.reshape(1).astype(jnp.int32), mine, others, grad_proj, grad_swap, lines
    )
    a2, a1, a3 = tied(turned(m2, 0, 2), turned(m1, 0, 1), turned(m3, 0, 3))
    total = keep + a1 + a2 + a3
    piece = total[:small]
    line = total[small, :rows].reshape(2, part)
    a2, a1, a3 = tied(*(turned(piece, 1, k) for k in STEPS))
    piece = (piece + a2) + (a1 + a3)
    given = shifted(jnp.where(c == 0, line[1], line[0]), "c", 1)
    loss_rows, loss_cols = jnp.where(c == 0, given, line[1]), jnp.where(c == 0, line[0], given)
    loss_far = crossed(loss_cols, 1, 0)
    loss_near = crossed(jnp.where(m == 0, loss_rows, loss_far), 0, 1)
    upper = jnp.logical_and(t == 1, m == 1)
    lower = jnp.logical_and(t == 1, m == 0)
    row_loss = (
        jnp.where(lower, 0.0, loss_rows)
        + jnp.where(upper, 0.0, loss_far)
        + jnp.where(t == 1, loss_near, 0.0)
    ) / pairs
    row_loss, piece = tied(row_loss, piece)
    p2, p1, p3, first = tied(*(turned(piece, 0, k) for k in STEPS), shifted(piece, "c", 1))
    pieces = [piece, p1, p3, p2]
    swapped = [shifted(v, "c", 1) for v in pieces[1:]]
    places = [c * half + (lead - k) % 4 * small for k in (0, 1, 3, 2)]
    others = [(1 - c) * half + (back - k) % 4 * small for k in (0, 1, 3, 2)]
    weight_grad = placed_rows(places + others[:1], pieces + [first], None)
    *swapped, weight_grad = tied(*swapped, weight_grad)
    weight_grad = placed_rows(others[1:], swapped, weight_grad)
    return (row_loss[None], weight_grad[None])


def pack_kernel(embed_ref, *refs):
    refs, out_refs = refs[:-2], refs[-2:]
    part, width = embed_ref.shape
    half = width // 2
    total = jnp.zeros((part, 128), F32)
    for k in range(2):
        here = pl.ds(k * half, half)
        grad = sum(ref[:, here].astype(F32) for ref in refs)
        product = grad * embed_ref[:, here].astype(F32)
        total += sum(product[:, i * 128 : (i + 1) * 128] for i in range(half // 128))
        out_refs[k][:part, :] = grad.astype(BF16)
    line = jnp.sum(total.T, axis=0, keepdims=True)
    parts = []
    for _ in range(3):
        parts.append(line.astype(BF16).astype(F32))
        line = line - parts[-1]
    extra = jnp.broadcast_to(jnp.concatenate(parts, axis=1), (EXTRA, 3 * part)).astype(BF16)
    for k in range(2):
        out_refs[k][part:, :] = extra


def packed(embed, *grads):
    part, width = embed.shape
    out = [pltpu.HBM((part + EXTRA, width // 2), BF16)] * 2
    return staged(pack_kernel, (), (embed,) + grads, out, 6 * part * width)


def unpack_kernel(flags_ref, scale_ref, p00, p10, p01, p11, projected_ref, inverse_ref, out_ref):
    part = p00.shape[0] - EXTRA
    t, m = flags_ref[0], flags_ref[1]
    scale = scale_ref[0]

    def finish(first, second, here):
        grad = first[:part, :].astype(F32) + second[:part, :].astype(F32)
        line = first[part : part + 1, :].astype(F32) + second[part : part + 1, :].astype(F32)
        line = line[:, :part] + line[:, part : 2 * part] + line[:, 2 * part :]
        along = jnp.broadcast_to(line, (128, part)).T[:, :1]
        inverse = inverse_ref[here, :]
        result = inverse * scale * (grad - inverse * along * projected_ref[here, :])
        out_ref[here, :] = result.astype(BF16)

    low, high = pl.ds(0, part), pl.ds(part, part)

    @pl.when(jnp.logical_and(t == 0, m == 0))
    def _():
        finish(p00, p10, low)
        finish(p01, p11, high)

    @pl.when(jnp.logical_and(t == 0, m == 1))
    def _():
        finish(p01, p11, low)
        finish(p00, p10, high)

    @pl.when(t == 1)
    def _():
        finish(p10, p11, low)
        finish(p00, p01, high)


def unpacked(flags, scale, pieces, projected, inverse):
    out = jax.ShapeDtypeStruct(projected.shape, BF16)
    operands = (*pieces, projected, inverse)
    return staged(unpack_kernel, (flags, scale), operands, out, 6 * projected.size, held=True)


def turned(value, late, step):
    route = []
    for i in range(32):
        x, y, c = i // 8, i // 2 % 4, i % 2
        if c ^ late:
            y = (y + step) % 4
        else:
            x = (x + step) % 4
        route.append((i, x * 8 + y * 2 + c))
    return lax.ppermute(value, ("x", "y", "c"), route)


def weight_kernel(lead_ref, mine, others, own_grad, other_grad, lines, *refs):
    *outs, total_ref = refs
    small = outs[0].shape[0] - lines.shape[1]
    total_ref[...] = lax.dot_general(
        mine[...], own_grad[...], (((0,), (0,)), ((), ())), preferred_element_type=F32
    ) + lax.dot_general(
        others[...], other_grad[...], (((0,), (0,)), ((), ())), preferred_element_type=F32
    )
    for k, out in enumerate(outs):
        here = pl.multiple_of((lead_ref[0] + k) % 4 * small, small)
        out[:small, :] = total_ref[pl.ds(here, small), :]
        out[small:, :] = lines[LINES[k]]


def weight_messages(lead, mine, others, own_grad, other_grad, lines):
    half = mine.shape[1]
    small = half // 4
    vmem = pl.BlockSpec(memory_space=pltpu.VMEM)
    message = jax.ShapeDtypeStruct((small + lines.shape[1], half), F32)
    return pl.pallas_call(
        weight_kernel,
        in_specs=[pl.BlockSpec(memory_space=pltpu.SMEM)] + [vmem] * 5,
        out_specs=[vmem] * 4,
        out_shape=[message] * 4,
        scratch_shapes=[pltpu.VMEM((half, half), F32)],
        compiler_params=pltpu.CompilerParams(vmem_limit_bytes=14 * 2**20),
        cost_estimate=pl.CostEstimate(
            flops=4 * mine.size * half, bytes_accessed=8 * mine.size, transcendentals=0
        ),
    )(lead, mine, others, own_grad, other_grad, lines)


def place_kernel(count, places_ref, *refs):
    pieces, out_ref, sems = refs[:count], refs[-2], refs[-1]
    copies = []
    for i, piece in enumerate(pieces):
        size = piece.shape[0]
        here = pl.ds(pl.multiple_of(places_ref[i], size), size)
        copies.append(pltpu.make_async_copy(piece, out_ref.at[here, :], sems.at[i]))
        copies[-1].start()
    for copy in copies:
        copy.wait()


def placed_rows(places, pieces, target):
    size, width = pieces[0].shape
    count = len(pieces)
    operands = in_hbm(pieces)
    specs = [pl.BlockSpec(memory_space=pltpu.VMEM)] * count
    if target is not None:
        operands += in_hbm([target])
        specs += [pl.BlockSpec(memory_space=pltpu.HBM)]
    return pl.pallas_call(
        functools.partial(place_kernel, count),
        in_specs=[pl.BlockSpec(memory_space=pltpu.SMEM)] + specs,
        out_specs=pl.BlockSpec(memory_space=pltpu.HBM),
        out_shape=pltpu.HBM((8 * size, width), F32),
        scratch_shapes=[pltpu.SemaphoreType.DMA((count,))],
        input_output_aliases={} if target is None else {count + 1: 0},
        compiler_params=pltpu.CompilerParams(vmem_limit_bytes=10 * 2**20),
    )(jnp.stack(places).astype(jnp.int32), *operands)


def solution(mesh):
    fine = Mesh(mesh.devices.reshape(4, 4, 2, 2, 2), ("x", "y", "c", "m", "t"))
    dp = ("x", "y", "c")
    placed = (P("t", dp, None), P("t", None, "m"), P(), P())
    return jax.shard_map(
        on_device,
        mesh=fine,
        in_specs=placed,
        out_specs=(P("t", dp + ("m",)), P("t", None, "m")),
        check_vma=False,
    )
```

```python
import functools
import math

import jax
import jax.numpy as jnp
from jax import lax
from jax.experimental import pallas as pl
from jax.experimental.pallas import tpu as pltpu
from jax.sharding import Mesh, PartitionSpec as P

F32 = jnp.float32
BF16 = jnp.bfloat16
STEPS = (2, 1, 3)
EXTRA = 16
LINES = (0, 2, 3, 1)


def shifted(value, axis, step):
    count = lax.axis_size(axis)
    return lax.ppermute(value, axis, [(i, (i + step) % count) for i in range(count)])


def crossed(value, tower, half):
    flip = 2 * half + tower
    return lax.ppermute(value, ("m", "t"), [(i, i ^ flip) for i in range(4)])


def pick(block, index, size, axis=0):
    return lax.dynamic_slice_in_dim(block, index * size, size, axis)


def tied(*values):
    return lax.optimization_barrier(values)


def in_hbm(values):
    return [pltpu.with_memory_space_constraint(v, pltpu.HBM) for v in values]


def tile_kernel(row_acc, col_acc, row_types, diagonal, *refs):
    refs = list(refs)
    n_rows, n_pairs = len(row_acc), len(col_acc)

    def take(count):
        return [refs.pop(0) for _ in range(count)]

    diag_ref, scale_ref = take(2)
    rows_refs = take(n_rows)
    cols_refs = [take(2) for _ in range(n_pairs)]
    row_sums = [refs.pop(0) if has else None for has in row_acc]
    col_sums = [take(2) if has else None for has in col_acc]
    ga_refs, gb_refs = take(n_rows), take(2 * n_pairs)
    la_ref, lb_ref, acc_ref, loss_ref = take(4)
    part, width = rows_refs[0].shape
    scale = scale_ref[0]
    bias = scale_ref[1]

    def products(step, r, core):
        return lax.dot_general(
            rows_refs[r][...],
            cols_refs[step][core][...],
            (((1,), (1,)), ((), ())),
            preferred_element_type=F32,
        )

    order = [(k, r, core) for k in range(n_pairs) for r in range(n_rows) for core in range(2)]
    coming = products(*order[0])
    for i, (step, r, core) in enumerate(order):
        logits = coming * scale + bias
        if i + 1 < len(order):
            coming = products(*order[i + 1])
        here = pl.ds(r * part, part)
        if r == 0 and core == 0:
            gb = [jnp.zeros((part, width), F32) for _ in range(2)]
        if core == 0:
            grad = jnp.zeros((part, width), F32)
        meets = diagonal and i == 0
        if meets:
            image = lax.broadcasted_iota(jnp.int32, (part, part), 0)
            text = lax.broadcasted_iota(jnp.int32, (part, part), 1)
            same = image + diag_ref[0] == text
            logits = jnp.where(same, -logits, logits)
        grown = jnp.exp2(logits)
        whole = 1.0 + grown
        inverse = pl.reciprocal(whole, approx=True)
        inverse = inverse * (2.0 - whole * inverse)
        losses = jnp.log(whole) + (grown - (whole - 1.0)) * inverse
        share = grown * inverse
        if meets:
            share = jnp.where(same, -share, share)
        coefficient = share.astype(BF16)
        folded = sum(losses[:, k * 128 : (k + 1) * 128] for k in range(part // 128))
        column = jnp.sum(losses, axis=0, keepdims=True)
        if step == 0 and core == 0:
            loss_ref[here, :] = folded
        else:
            loss_ref[here, :] += folded
        if r == 0:
            lb_ref[2 * step + core] = column
        else:
            lb_ref[2 * step + core] += column
        grad += jnp.dot(coefficient, cols_refs[step][core][...], preferred_element_type=F32)
        gb[core] += lax.dot_general(
            coefficient, rows_refs[r][...], (((0,), (0,)), ((), ())), preferred_element_type=F32
        )
        if core == 1:
            if step == 0 and row_acc[r]:
                grad += row_sums[r][...]
            if step > 0:
                grad += acc_ref[here, :]
            if step < n_pairs - 1:
                acc_ref[here, :] = grad
            else:
                ga_refs[r][...] = grad.astype(row_types[r])
        if r == n_rows - 1:
            total = gb[core]
            if col_acc[step]:
                total += col_sums[step][core][...]
            gb_refs[2 * step + core][...] = total.astype(gb_refs[2 * step + core].dtype)
    for r in range(n_rows):
        la_ref[r] = jnp.sum(loss_ref[pl.ds(r * part, part), :].T, axis=0, keepdims=True)


def tile_terms(rows, cols, row_sums, col_sums, row_types, col_types, diagonal, diag, scales, far=()):
    part, width = rows[0].shape
    n_rows, n_pairs = len(rows), len(cols)
    smem = pl.BlockSpec(memory_space=pltpu.SMEM)
    vmem = pl.BlockSpec(memory_space=pltpu.VMEM)
    operands = list(rows) + [v for pair in cols for v in pair]
    held = set(map(id, far))
    operands = [v if id(v) in held else in_hbm([v])[0] for v in operands]
    operands += [v for v in row_sums if v is not None]
    operands += [v for pair in col_sums if pair is not None for v in pair]
    body = functools.partial(
        tile_kernel,
        [v is not None for v in row_sums],
        [v is not None for v in col_sums],
        row_types,
        diagonal,
    )
    kinds = list(row_types) + [kind for kind in col_types for _ in range(2)]
    out_shape = [
        jax.ShapeDtypeStruct((part, width), F32) if kind == F32 else pltpu.HBM((part, width), kind)
        for kind in kinds
    ]
    n_out = len(out_shape)
    out_shape += [jax.ShapeDtypeStruct((n, 1, part), F32) for n in (n_rows, 2 * n_pairs)]
    out = pl.pallas_call(
        body,
        in_specs=[smem, smem] + [vmem] * len(operands),
        out_specs=[vmem] * len(out_shape),
        out_shape=out_shape,
        scratch_shapes=[
            pltpu.VMEM((n_rows * part if n_pairs > 1 else 8, width), F32),
            pltpu.VMEM((n_rows * part, 128), F32),
        ],
        compiler_params=pltpu.CompilerParams(vmem_limit_bytes=32 * 2**20),
        cost_estimate=pl.CostEstimate(
            flops=6 * n_rows * 2 * n_pairs * part * part * width,
            bytes_accessed=2 * 2 * (n_rows + 2 * n_pairs) * part * width,
            transcendentals=3 * 2 * n_rows * n_pairs * part * part,
        ),
    )(diag, scales, *operands)
    grad_rows, grad_cols = out[:n_rows], out[n_rows:n_out]
    return grad_rows, grad_cols, out[-2].reshape(n_rows, part), out[-1].reshape(n_pairs, 2, part)


def staged(body, smalls, operands, out_shape, cost, held=False):
    vmem = pl.BlockSpec(memory_space=pltpu.VMEM)
    return pl.pallas_call(
        body,
        in_specs=[pl.BlockSpec(memory_space=pltpu.SMEM)] * len(smalls) + [vmem] * len(operands),
        out_specs=jax.tree.map(lambda _: vmem, out_shape),
        out_shape=out_shape,
        compiler_params=pltpu.CompilerParams(vmem_limit_bytes=10 * 2**20),
        cost_estimate=pl.CostEstimate(flops=cost, bytes_accessed=2 * cost, transcendentals=0),
    )(*smalls, *(in_hbm(operands) if held else operands))


def on_device(features, projection, similarity_scale, logit_bias):
    x, y, c = lax.axis_index("x"), lax.axis_index("y"), lax.axis_index("c")
    m, t = lax.axis_index("m"), lax.axis_index("t")
    inputs = features[0]
    rows, width = inputs.shape
    weight = projection[0]
    half = weight.shape[1]
    part = rows // 2
    pairs = rows * 32
    scale_factor = similarity_scale[0]

    projected = jnp.dot(inputs, weight, preferred_element_type=F32)
    squares = lax.psum(jnp.sum(projected * projected, axis=1), "m")[:, None]
    inverse = lax.rsqrt(squares + 1e-06)
    embedded = (projected * inverse).astype(BF16)
    mine = pick(inputs, c, half, 1)
    others = shifted(pick(inputs, 1 - c, half, 1), "c", 1)

    def rows_for(tower, flip):
        return pick(embedded, jnp.where(t == 0, m ^ flip, 1 ^ tower), part)

    kept = rows_for(0, 0)
    far, near, cross = tied(
        crossed(rows_for(1, 0), 1, 0), crossed(rows_for(0, 1), 0, 1), crossed(rows_for(1, 1), 1, 1)
    )
    own = jnp.concatenate([kept, near], axis=1)
    other = jnp.concatenate([far, cross], axis=1)
    own, other = tied(own, other)

    r1, r3, c1, c3, d0 = tied(
        shifted(own, "y", 1),
        shifted(own, "y", 3),
        shifted(other, "x", 1),
        shifted(other, "x", 3),
        shifted(other, "c", 1),
    )
    c2, r2 = shifted(other, "x", 2), shifted(own, "y", 2)
    d1, d3 = shifted(c1, "c", 1), shifted(c3, "c", 1)
    diag = jnp.where(m == t, 0, 2 * part).astype(jnp.int32).reshape(1)
    scales = jnp.stack([scale_factor, logit_bias[0]]) * math.log2(math.e)
    near = [own, r1, r3]
    cols0, cols1, cols3 = [other, d0], [c1, d1], [c3, d3]
    rows_sum, (a0, b0, a1, b1, a3, b3), la, lb = tile_terms(
        near,
        [cols0, cols1, cols3],
        [None] * 3,
        [None] * 3,
        [F32] * 3,
        [F32] * 3,
        True,
        diag,
        scales,
    )
    c2, r2, a0, b0, a1, b1, a3, b3, *rows_sum = tied(c2, r2, a0, b0, a1, b1, a3, b3, *rows_sum)
    d2 = shifted(c2, "c", 1)
    (sum2,), (s1, t1, s3, t3), la2, lb2 = tile_terms(
        [r2],
        [cols1, cols3],
        [None],
        [[a1, b1], [a3, b3]],
        [F32],
        [BF16] * 2,
        False,
        diag,
        scales,
        [r2],
    )
    t1, t3 = shifted(t1, "c", 1), shifted(t3, "c", 1)
    (g2,), (s0, t0, a2, b2), la4, lb4 = tile_terms(
        [r2],
        [cols0, [c2, d2]],
        [sum2],
        [[a0, b0], None],
        [BF16],
        [BF16, F32],
        False,
        diag,
        scales,
        [r2, c2, d2],
    )
    t1, t3, g2, s0, t0, a2, b2 = tied(t1, t3, g2, s0, t0, a2, b2)

    def joined(a, b):
        return (a.astype(F32) + b.astype(F32)).astype(BF16)

    s1, s3, a2, b2 = tied(joined(s1, t1), joined(s3, t3), a2, b2)
    e1, e3 = shifted(s1, "x", 3), shifted(s3, "x", 1)
    f2 = shifted(g2, "y", 2)
    t0 = shifted(t0, "c", 1)
    (g0, g1, g3), (s2, t2), la3, lb3 = tile_terms(
        near,
        [[c2, d2]],
        rows_sum,
        [[a2, b2]],
        [BF16] * 3,
        [BF16],
        False,
        diag,
        scales,
        [c2, d2],
    )
    loss_rows = jnp.concatenate([la + la3, la2 + la4])
    loss_cols = jnp.stack([lb[0] + lb4[0], lb[1] + lb2[0], lb[2] + lb2[1], lb4[1] + lb3[0]], axis=1)
    e1, e3, f2, t0, g0, g1, g3, s2, t2 = tied(e1, e3, f2, t0, g0, g1, g3, s2, t2)
    s2 = joined(s2, shifted(t2, "c", 1))
    f1, f3 = shifted(g1, "y", 3), shifted(g3, "y", 1)
    e2 = shifted(s2, "x", 2)
    e2, f1, f3 = tied(e2, f1, f3)
    own0, own1 = packed(own, g0, f1, f2, f3)
    other0, other1 = packed(other, s0, t0, e1, e2, e3)
    far, near, cross = tied(crossed(other0, 1, 0), crossed(own1, 0, 1), crossed(other1, 1, 1))
    flags = jnp.stack([t, m]).astype(jnp.int32)
    scale = (scale_factor / pairs).reshape(1)
    grad_proj = unpacked(flags, scale, [own0, far, near, cross], projected, inverse)

    given = shifted(
        jnp.where(c == 0, jnp.stack([loss_rows, loss_rows]), loss_cols), "c", 1
    )
    losses = jnp.where(c == 0, loss_cols + given[::-1], jnp.stack([given[0], loss_rows]))
    losses, grad_proj = tied(losses, grad_proj)
    lines = losses.transpose(1, 0, 2).reshape(4, 1, rows)
    lines = jnp.pad(lines, ((0, 0), (0, 7), (0, half - rows)))

    grad_swap = shifted(grad_proj, "c", 1)
    small = half // 4
    lead = jnp.where(c == 0, x, y)
    back = jnp.where(c == 0, y, x)
    keep, m1, m2, m3 = weight_messages(
        lead.reshape(1).astype(jnp.int32), mine, others, grad_proj, grad_swap, lines
    )
    a2, a1, a3 = tied(turned(m2, 0, 2), turned(m1, 0, 1), turned(m3, 0, 3))
    total = keep + a1 + a2 + a3
    piece = total[:small]
    line = total[small, :rows].reshape(2, part)
    a2, a1, a3 = tied(*(turned(piece, 1, k) for k in STEPS))
    piece = (piece + a2) + (a1 + a3)
    given = shifted(jnp.where(c == 0, line[1], line[0]), "c", 1)
    loss_rows, loss_cols = jnp.where(c == 0, given, line[1]), jnp.where(c == 0, line[0], given)
    loss_far = crossed(loss_cols, 1, 0)
    loss_near = crossed(jnp.where(m == 0, loss_rows, loss_far), 0, 1)
    upper = jnp.logical_and(t == 1, m == 1)
    lower = jnp.logical_and(t == 1, m == 0)
    row_loss = (
        jnp.where(lower, 0.0, loss_rows)
        + jnp.where(upper, 0.0, loss_far)
        + jnp.where(t == 1, loss_near, 0.0)
    ) / pairs
    row_loss, piece = tied(row_loss, piece)
    places = [c * half + (lead - k) % 4 * small for k in (0, 1, 3, 2)]
    others = [(1 - c) * half + (back - k) % 4 * small for k in (0, 1, 3, 2)]
    first = [piece, shifted(piece, "c", 1)]
    weight_grad = placed_rows(places[:1] + others[:1], first, None)
    p2, p1, p3, weight_grad = tied(*(turned(piece, 0, k) for k in STEPS), weight_grad)
    pieces = [piece, p1, p3, p2]
    swapped = [shifted(v, "c", 1) for v in pieces[1:]]
    weight_grad = placed_rows(places[1:], pieces[1:], weight_grad)
    *swapped, weight_grad = tied(*swapped, weight_grad)
    weight_grad = placed_rows(others[1:], swapped, weight_grad)
    return (row_loss[None], weight_grad[None])


def pack_kernel(embed_ref, *refs):
    refs, out_refs = refs[:-2], refs[-2:]
    part, width = embed_ref.shape
    half = width // 2
    total = jnp.zeros((part, 128), F32)
    for k in range(2):
        here = pl.ds(k * half, half)
        grad = sum(ref[:, here].astype(F32) for ref in refs)
        product = grad * embed_ref[:, here].astype(F32)
        total += sum(product[:, i * 128 : (i + 1) * 128] for i in range(half // 128))
        out_refs[k][:part, :] = grad.astype(BF16)
    line = jnp.sum(total.T, axis=0, keepdims=True)
    parts = []
    for _ in range(3):
        parts.append(line.astype(BF16).astype(F32))
        line = line - parts[-1]
    extra = jnp.broadcast_to(jnp.concatenate(parts, axis=1), (EXTRA, 3 * part)).astype(BF16)
    for k in range(2):
        out_refs[k][part:, :] = extra


def packed(embed, *grads):
    part, width = embed.shape
    out = [pltpu.HBM((part + EXTRA, width // 2), BF16)] * 2
    return staged(pack_kernel, (), (embed,) + grads, out, 6 * part * width)


def unpack_kernel(flags_ref, scale_ref, p00, p10, p01, p11, projected_ref, inverse_ref, out_ref):
    part = p00.shape[0] - EXTRA
    t, m = flags_ref[0], flags_ref[1]
    scale = scale_ref[0]

    def finish(first, second, here):
        grad = first[:part, :].astype(F32) + second[:part, :].astype(F32)
        line = first[part : part + 1, :].astype(F32) + second[part : part + 1, :].astype(F32)
        line = line[:, :part] + line[:, part : 2 * part] + line[:, 2 * part :]
        along = jnp.broadcast_to(line, (128, part)).T[:, :1]
        inverse = inverse_ref[here, :]
        result = inverse * scale * (grad - inverse * along * projected_ref[here, :])
        out_ref[here, :] = result.astype(BF16)

    low, high = pl.ds(0, part), pl.ds(part, part)

    @pl.when(jnp.logical_and(t == 0, m == 0))
    def _():
        finish(p00, p10, low)
        finish(p01, p11, high)

    @pl.when(jnp.logical_and(t == 0, m == 1))
    def _():
        finish(p01, p11, low)
        finish(p00, p10, high)

    @pl.when(t == 1)
    def _():
        finish(p10, p11, low)
        finish(p00, p01, high)


def unpacked(flags, scale, pieces, projected, inverse):
    out = jax.ShapeDtypeStruct(projected.shape, BF16)
    operands = (*pieces, projected, inverse)
    return staged(unpack_kernel, (flags, scale), operands, out, 6 * projected.size, held=True)


def turned(value, late, step):
    route = []
    for i in range(32):
        x, y, c = i // 8, i // 2 % 4, i % 2
        if c ^ late:
            y = (y + step) % 4
        else:
            x = (x + step) % 4
        route.append((i, x * 8 + y * 2 + c))
    return lax.ppermute(value, ("x", "y", "c"), route)


def weight_kernel(lead_ref, mine, others, own_grad, other_grad, lines, *refs):
    *outs, total_ref = refs
    small = outs[0].shape[0] - lines.shape[1]
    total_ref[...] = lax.dot_general(
        mine[...], own_grad[...], (((0,), (0,)), ((), ())), preferred_element_type=F32
    ) + lax.dot_general(
        others[...], other_grad[...], (((0,), (0,)), ((), ())), preferred_element_type=F32
    )
    for k, out in enumerate(outs):
        here = pl.multiple_of((lead_ref[0] + k) % 4 * small, small)
        out[:small, :] = total_ref[pl.ds(here, small), :]
        out[small:, :] = lines[LINES[k]]


def weight_messages(lead, mine, others, own_grad, other_grad, lines):
    half = mine.shape[1]
    small = half // 4
    vmem = pl.BlockSpec(memory_space=pltpu.VMEM)
    message = jax.ShapeDtypeStruct((small + lines.shape[1], half), F32)
    return pl.pallas_call(
        weight_kernel,
        in_specs=[pl.BlockSpec(memory_space=pltpu.SMEM)] + [vmem] * 5,
        out_specs=[vmem] * 4,
        out_shape=[message] * 4,
        scratch_shapes=[pltpu.VMEM((half, half), F32)],
        compiler_params=pltpu.CompilerParams(vmem_limit_bytes=14 * 2**20),
        cost_estimate=pl.CostEstimate(
            flops=4 * mine.size * half, bytes_accessed=8 * mine.size, transcendentals=0
        ),
    )(lead, mine, others, own_grad, other_grad, lines)


def place_kernel(count, places_ref, *refs):
    pieces, out_ref, sems = refs[:count], refs[-2], refs[-1]
    copies = []
    for i, piece in enumerate(pieces):
        size = piece.shape[0]
        here = pl.ds(pl.multiple_of(places_ref[i], size), size)
        copies.append(pltpu.make_async_copy(piece, out_ref.at[here, :], sems.at[i]))
        copies[-1].start()
    for copy in copies:
        copy.wait()


def placed_rows(places, pieces, target):
    size, width = pieces[0].shape
    count = len(pieces)
    operands = list(pieces)
    specs = [pl.BlockSpec(memory_space=pltpu.VMEM)] * count
    if target is not None:
        operands += in_hbm([target])
        specs += [pl.BlockSpec(memory_space=pltpu.HBM)]
    return pl.pallas_call(
        functools.partial(place_kernel, count),
        in_specs=[pl.BlockSpec(memory_space=pltpu.SMEM)] + specs,
        out_specs=pl.BlockSpec(memory_space=pltpu.HBM),
        out_shape=pltpu.HBM((8 * size, width), F32),
        scratch_shapes=[pltpu.SemaphoreType.DMA((count,))],
        input_output_aliases={} if target is None else {count + 1: 0},
        compiler_params=pltpu.CompilerParams(vmem_limit_bytes=10 * 2**20),
    )(jnp.stack(places).astype(jnp.int32), *operands)


def solution(mesh):
    fine = Mesh(mesh.devices.reshape(4, 4, 2, 2, 2), ("x", "y", "c", "m", "t"))
    dp = ("x", "y", "c")
    placed = (P("t", dp, None), P("t", None, "m"), P(), P())
    return jax.shard_map(
        on_device,
        mesh=fine,
        in_specs=placed,
        out_specs=(P("t", dp + ("m",)), P("t", None, "m")),
        check_vma=False,
    )
```

```python
import functools
import math

import jax
import jax.numpy as jnp
from jax import lax
from jax.experimental import pallas as pl
from jax.experimental.pallas import tpu as pltpu
from jax.sharding import Mesh, PartitionSpec as P

F32 = jnp.float32
BF16 = jnp.bfloat16
STEPS = (2, 1, 3)
EXTRA = 16
LINES = (0, 2, 3, 1)


def shifted(value, axis, step):
    count = lax.axis_size(axis)
    return lax.ppermute(value, axis, [(i, (i + step) % count) for i in range(count)])


def crossed(value, tower, half):
    flip = 2 * half + tower
    return lax.ppermute(value, ("m", "t"), [(i, i ^ flip) for i in range(4)])


def pick(block, index, size, axis=0):
    return lax.dynamic_slice_in_dim(block, index * size, size, axis)


def tied(*values):
    return lax.optimization_barrier(values)


def in_hbm(values):
    return [pltpu.with_memory_space_constraint(v, pltpu.HBM) for v in values]


def tile_kernel(row_acc, col_acc, row_types, diagonal, *refs):
    refs = list(refs)
    n_rows, n_pairs = len(row_acc), len(col_acc)

    def take(count):
        return [refs.pop(0) for _ in range(count)]

    diag_ref, scale_ref = take(2)
    rows_refs = take(n_rows)
    cols_refs = [take(2) for _ in range(n_pairs)]
    row_sums = [refs.pop(0) if has else None for has in row_acc]
    col_sums = [take(2) if has else None for has in col_acc]
    ga_refs, gb_refs = take(n_rows), take(2 * n_pairs)
    la_ref, lb_ref, acc_ref, loss_ref = take(4)
    part, width = rows_refs[0].shape
    scale = scale_ref[0]
    bias = scale_ref[1]

    def products(step, r, core):
        return lax.dot_general(
            rows_refs[r][...],
            cols_refs[step][core][...],
            (((1,), (1,)), ((), ())),
            preferred_element_type=F32,
        )

    order = [(k, r, core) for k in range(n_pairs) for r in range(n_rows) for core in range(2)]
    coming = products(*order[0])
    for i, (step, r, core) in enumerate(order):
        logits = coming * scale + bias
        if i + 1 < len(order):
            coming = products(*order[i + 1])
        here = pl.ds(r * part, part)
        if r == 0 and core == 0:
            gb = [jnp.zeros((part, width), F32) for _ in range(2)]
        if core == 0:
            grad = jnp.zeros((part, width), F32)
        meets = diagonal and i == 0
        if meets:
            image = lax.broadcasted_iota(jnp.int32, (part, part), 0)
            text = lax.broadcasted_iota(jnp.int32, (part, part), 1)
            same = image + diag_ref[0] == text
            logits = jnp.where(same, -logits, logits)
        grown = jnp.exp2(logits)
        whole = 1.0 + grown
        inverse = pl.reciprocal(whole, approx=True)
        inverse = inverse * (2.0 - whole * inverse)
        losses = jnp.log(whole) + (grown - (whole - 1.0)) * inverse
        share = grown * inverse
        if meets:
            share = jnp.where(same, -share, share)
        coefficient = share.astype(BF16)
        folded = sum(losses[:, k * 128 : (k + 1) * 128] for k in range(part // 128))
        column = jnp.sum(losses, axis=0, keepdims=True)
        if step == 0 and core == 0:
            loss_ref[here, :] = folded
        else:
            loss_ref[here, :] += folded
        if r == 0:
            lb_ref[2 * step + core] = column
        else:
            lb_ref[2 * step + core] += column
        grad += jnp.dot(coefficient, cols_refs[step][core][...], preferred_element_type=F32)
        gb[core] += lax.dot_general(
            coefficient, rows_refs[r][...], (((0,), (0,)), ((), ())), preferred_element_type=F32
        )
        if core == 1:
            if step == 0 and row_acc[r]:
                grad += row_sums[r][...]
            if step > 0:
                grad += acc_ref[here, :]
            if step < n_pairs - 1:
                acc_ref[here, :] = grad
            else:
                ga_refs[r][...] = grad.astype(row_types[r])
        if r == n_rows - 1:
            total = gb[core]
            if col_acc[step]:
                total += col_sums[step][core][...]
            gb_refs[2 * step + core][...] = total.astype(gb_refs[2 * step + core].dtype)
    for r in range(n_rows):
        la_ref[r] = jnp.sum(loss_ref[pl.ds(r * part, part), :].T, axis=0, keepdims=True)


def tile_terms(rows, cols, row_sums, col_sums, row_types, col_types, diagonal, diag, scales, far=()):
    part, width = rows[0].shape
    n_rows, n_pairs = len(rows), len(cols)
    smem = pl.BlockSpec(memory_space=pltpu.SMEM)
    vmem = pl.BlockSpec(memory_space=pltpu.VMEM)
    operands = list(rows) + [v for pair in cols for v in pair]
    held = set(map(id, far))
    operands = [v if id(v) in held else in_hbm([v])[0] for v in operands]
    operands += [v for v in row_sums if v is not None]
    operands += [v for pair in col_sums if pair is not None for v in pair]
    body = functools.partial(
        tile_kernel,
        [v is not None for v in row_sums],
        [v is not None for v in col_sums],
        row_types,
        diagonal,
    )
    kinds = list(row_types) + [kind for kind in col_types for _ in range(2)]
    out_shape = [
        jax.ShapeDtypeStruct((part, width), F32) if kind == F32 else pltpu.HBM((part, width), kind)
        for kind in kinds
    ]
    n_out = len(out_shape)
    out_shape += [jax.ShapeDtypeStruct((n, 1, part), F32) for n in (n_rows, 2 * n_pairs)]
    out = pl.pallas_call(
        body,
        in_specs=[smem, smem] + [vmem] * len(operands),
        out_specs=[vmem] * len(out_shape),
        out_shape=out_shape,
        scratch_shapes=[
            pltpu.VMEM((n_rows * part if n_pairs > 1 else 8, width), F32),
            pltpu.VMEM((n_rows * part, 128), F32),
        ],
        compiler_params=pltpu.CompilerParams(vmem_limit_bytes=32 * 2**20),
        cost_estimate=pl.CostEstimate(
            flops=6 * n_rows * 2 * n_pairs * part * part * width,
            bytes_accessed=2 * 2 * (n_rows + 2 * n_pairs) * part * width,
            transcendentals=3 * 2 * n_rows * n_pairs * part * part,
        ),
    )(diag, scales, *operands)
    grad_rows, grad_cols = out[:n_rows], out[n_rows:n_out]
    return grad_rows, grad_cols, out[-2].reshape(n_rows, part), out[-1].reshape(n_pairs, 2, part)


def staged(body, smalls, operands, out_shape, cost, held=False):
    vmem = pl.BlockSpec(memory_space=pltpu.VMEM)
    return pl.pallas_call(
        body,
        in_specs=[pl.BlockSpec(memory_space=pltpu.SMEM)] * len(smalls) + [vmem] * len(operands),
        out_specs=jax.tree.map(lambda _: vmem, out_shape),
        out_shape=out_shape,
        compiler_params=pltpu.CompilerParams(vmem_limit_bytes=10 * 2**20),
        cost_estimate=pl.CostEstimate(flops=cost, bytes_accessed=2 * cost, transcendentals=0),
    )(*smalls, *(in_hbm(operands) if held else operands))


def on_device(features, projection, similarity_scale, logit_bias):
    x, y, c = lax.axis_index("x"), lax.axis_index("y"), lax.axis_index("c")
    m, t = lax.axis_index("m"), lax.axis_index("t")
    inputs = features[0]
    rows, width = inputs.shape
    weight = projection[0]
    half = weight.shape[1]
    part = rows // 2
    pairs = rows * 32
    scale_factor = similarity_scale[0]

    projected = jnp.dot(inputs, weight, preferred_element_type=F32)
    squares = lax.psum(jnp.sum(projected * projected, axis=1), "m")[:, None]
    inverse = lax.rsqrt(squares + 1e-06)
    embedded = (projected * inverse).astype(BF16)
    mine = pick(inputs, c, half, 1)
    others = shifted(pick(inputs, 1 - c, half, 1), "c", 1)

    def rows_for(tower, flip):
        return pick(embedded, jnp.where(t == 0, m ^ flip, 1 ^ tower), part)

    kept = rows_for(0, 0)
    far, near, cross = tied(
        crossed(rows_for(1, 0), 1, 0), crossed(rows_for(0, 1), 0, 1), crossed(rows_for(1, 1), 1, 1)
    )
    own = jnp.concatenate([kept, near], axis=1)
    other = jnp.concatenate([far, cross], axis=1)
    own, other = tied(own, other)

    r1, r3, c1, c3 = tied(
        shifted(own, "y", 1),
        shifted(own, "y", 3),
        shifted(other, "x", 1),
        shifted(other, "x", 3),
    )
    d0 = shifted(other, "c", 1)
    c2, r2 = shifted(other, "x", 2), shifted(own, "y", 2)
    d1, d3 = shifted(c1, "c", 1), shifted(c3, "c", 1)
    diag = jnp.where(m == t, 0, 2 * part).astype(jnp.int32).reshape(1)
    scales = jnp.stack([scale_factor, logit_bias[0]]) * math.log2(math.e)
    near = [own, r1, r3]
    cols0, cols1, cols3 = [other, d0], [c1, d1], [c3, d3]
    rows_sum, (a0, b0, a1, b1, a3, b3), la, lb = tile_terms(
        near,
        [cols0, cols1, cols3],
        [None] * 3,
        [None] * 3,
        [F32] * 3,
        [F32] * 3,
        True,
        diag,
        scales,
    )
    c2, r2, a0, b0, a1, b1, a3, b3, *rows_sum = tied(c2, r2, a0, b0, a1, b1, a3, b3, *rows_sum)
    d2 = shifted(c2, "c", 1)
    (sum2,), (s1, t1, s3, t3), la2, lb2 = tile_terms(
        [r2],
        [cols1, cols3],
        [None],
        [[a1, b1], [a3, b3]],
        [F32],
        [BF16] * 2,
        False,
        diag,
        scales,
        [r2],
    )
    t1, t3 = shifted(t1, "c", 1), shifted(t3, "c", 1)
    (g2,), (s0, t0, a2, b2), la4, lb4 = tile_terms(
        [r2],
        [cols0, [c2, d2]],
        [sum2],
        [[a0, b0], None],
        [BF16],
        [BF16, F32],
        False,
        diag,
        scales,
        [r2, c2, d2],
    )
    t1, t3, g2, s0, t0, a2, b2 = tied(t1, t3, g2, s0, t0, a2, b2)

    def joined(a, b):
        return (a.astype(F32) + b.astype(F32)).astype(BF16)

    s1, s3, a2, b2 = tied(joined(s1, t1), joined(s3, t3), a2, b2)
    e1, e3 = shifted(s1, "x", 3), shifted(s3, "x", 1)
    f2 = shifted(g2, "y", 2)
    t0 = shifted(t0, "c", 1)
    (g0, g1, g3), (s2, t2), la3, lb3 = tile_terms(
        near,
        [[c2, d2]],
        rows_sum,
        [[a2, b2]],
        [BF16] * 3,
        [BF16],
        False,
        diag,
        scales,
        [c2, d2],
    )
    loss_rows = jnp.concatenate([la + la3, la2 + la4])
    loss_cols = jnp.stack([lb[0] + lb4[0], lb[1] + lb2[0], lb[2] + lb2[1], lb4[1] + lb3[0]], axis=1)
    e1, e3, f2, t0, g0, g1, g3, s2, t2 = tied(e1, e3, f2, t0, g0, g1, g3, s2, t2)
    s2 = joined(s2, shifted(t2, "c", 1))
    f1, f3 = shifted(g1, "y", 3), shifted(g3, "y", 1)
    e2 = shifted(s2, "x", 2)
    e2, f1, f3 = tied(e2, f1, f3)
    own0, own1 = packed(own, g0, f1, f2, f3)
    other0, other1 = packed(other, s0, t0, e1, e2, e3)
    far, near, cross = tied(crossed(other0, 1, 0), crossed(own1, 0, 1), crossed(other1, 1, 1))
    flags = jnp.stack([t, m]).astype(jnp.int32)
    scale = (scale_factor / pairs).reshape(1)
    grad_proj = unpacked(flags, scale, [own0, far, near, cross], projected, inverse)

    given = shifted(
        jnp.where(c == 0, jnp.stack([loss_rows, loss_rows]), loss_cols), "c", 1
    )
    losses = jnp.where(c == 0, loss_cols + given[::-1], jnp.stack([given[0], loss_rows]))
    losses, grad_proj = tied(losses, grad_proj)
    lines = losses.transpose(1, 0, 2).reshape(4, 1, rows)
    lines = jnp.pad(lines, ((0, 0), (0, 7), (0, half - rows)))

    grad_swap = shifted(grad_proj, "c", 1)
    small = half // 4
    lead = jnp.where(c == 0, x, y)
    back = jnp.where(c == 0, y, x)
    keep, m1, m2, m3 = weight_messages(
        lead.reshape(1).astype(jnp.int32), mine, others, grad_proj, grad_swap, lines
    )
    a2, a1, a3 = tied(turned(m2, 0, 2), turned(m1, 0, 1), turned(m3, 0, 3))
    total = keep + a1 + a2 + a3
    piece = total[:small]
    line = total[small, :rows].reshape(2, part)
    a2, a1, a3 = tied(*(turned(piece, 1, k) for k in STEPS))
    piece = (piece + a2) + (a1 + a3)
    given = shifted(jnp.where(c == 0, line[1], line[0]), "c", 1)
    loss_rows, loss_cols = jnp.where(c == 0, given, line[1]), jnp.where(c == 0, line[0], given)
    loss_far = crossed(loss_cols, 1, 0)
    loss_near = crossed(jnp.where(m == 0, loss_rows, loss_far), 0, 1)
    upper = jnp.logical_and(t == 1, m == 1)
    lower = jnp.logical_and(t == 1, m == 0)
    row_loss = (
        jnp.where(lower, 0.0, loss_rows)
        + jnp.where(upper, 0.0, loss_far)
        + jnp.where(t == 1, loss_near, 0.0)
    ) / pairs
    row_loss, piece = tied(row_loss, piece)
    places = [c * half + (lead - k) % 4 * small for k in (0, 1, 3, 2)]
    others = [(1 - c) * half + (back - k) % 4 * small for k in (0, 1, 3, 2)]
    first = [piece, shifted(piece, "c", 1)]
    weight_grad = placed_rows(places[:1] + others[:1], first, None)
    p2, p1, p3, weight_grad = tied(*(turned(piece, 0, k) for k in STEPS), weight_grad)
    pieces = [piece, p1, p3, p2]
    swapped = [shifted(v, "c", 1) for v in pieces[1:]]
    weight_grad = placed_rows(places[1:], pieces[1:], weight_grad)
    *swapped, weight_grad = tied(*swapped, weight_grad)
    weight_grad = placed_rows(others[1:], swapped, weight_grad)
    return (row_loss[None], weight_grad[None])


def pack_kernel(embed_ref, *refs):
    refs, out_refs = refs[:-2], refs[-2:]
    part, width = embed_ref.shape
    half = width // 2
    total = jnp.zeros((part, 128), F32)
    for k in range(2):
        here = pl.ds(k * half, half)
        grad = sum(ref[:, here].astype(F32) for ref in refs)
        product = grad * embed_ref[:, here].astype(F32)
        total += sum(product[:, i * 128 : (i + 1) * 128] for i in range(half // 128))
        out_refs[k][:part, :] = grad.astype(BF16)
    line = jnp.sum(total.T, axis=0, keepdims=True)
    parts = []
    for _ in range(3):
        parts.append(line.astype(BF16).astype(F32))
        line = line - parts[-1]
    extra = jnp.broadcast_to(jnp.concatenate(parts, axis=1), (EXTRA, 3 * part)).astype(BF16)
    for k in range(2):
        out_refs[k][part:, :] = extra


def packed(embed, *grads):
    part, width = embed.shape
    out = [pltpu.HBM((part + EXTRA, width // 2), BF16)] * 2
    return staged(pack_kernel, (), (embed,) + grads, out, 6 * part * width)


def unpack_kernel(flags_ref, scale_ref, p00, p10, p01, p11, projected_ref, inverse_ref, out_ref):
    part = p00.shape[0] - EXTRA
    t, m = flags_ref[0], flags_ref[1]
    scale = scale_ref[0]

    def finish(first, second, here):
        grad = first[:part, :].astype(F32) + second[:part, :].astype(F32)
        line = first[part : part + 1, :].astype(F32) + second[part : part + 1, :].astype(F32)
        line = line[:, :part] + line[:, part : 2 * part] + line[:, 2 * part :]
        along = jnp.broadcast_to(line, (128, part)).T[:, :1]
        inverse = inverse_ref[here, :]
        result = inverse * scale * (grad - inverse * along * projected_ref[here, :])
        out_ref[here, :] = result.astype(BF16)

    low, high = pl.ds(0, part), pl.ds(part, part)

    @pl.when(jnp.logical_and(t == 0, m == 0))
    def _():
        finish(p00, p10, low)
        finish(p01, p11, high)

    @pl.when(jnp.logical_and(t == 0, m == 1))
    def _():
        finish(p01, p11, low)
        finish(p00, p10, high)

    @pl.when(t == 1)
    def _():
        finish(p10, p11, low)
        finish(p00, p01, high)


def unpacked(flags, scale, pieces, projected, inverse):
    out = jax.ShapeDtypeStruct(projected.shape, BF16)
    operands = (*pieces, projected, inverse)
    return staged(unpack_kernel, (flags, scale), operands, out, 6 * projected.size, held=True)


def turned(value, late, step):
    route = []
    for i in range(32):
        x, y, c = i // 8, i // 2 % 4, i % 2
        if c ^ late:
            y = (y + step) % 4
        else:
            x = (x + step) % 4
        route.append((i, x * 8 + y * 2 + c))
    return lax.ppermute(value, ("x", "y", "c"), route)


def weight_kernel(lead_ref, mine, others, own_grad, other_grad, lines, *refs):
    *outs, total_ref = refs
    small = outs[0].shape[0] - lines.shape[1]
    total_ref[...] = lax.dot_general(
        mine[...], own_grad[...], (((0,), (0,)), ((), ())), preferred_element_type=F32
    ) + lax.dot_general(
        others[...], other_grad[...], (((0,), (0,)), ((), ())), preferred_element_type=F32
    )
    for k, out in enumerate(outs):
        here = pl.multiple_of((lead_ref[0] + k) % 4 * small, small)
        out[:small, :] = total_ref[pl.ds(here, small), :]
        out[small:, :] = lines[LINES[k]]


def weight_messages(lead, mine, others, own_grad, other_grad, lines):
    half = mine.shape[1]
    small = half // 4
    vmem = pl.BlockSpec(memory_space=pltpu.VMEM)
    message = jax.ShapeDtypeStruct((small + lines.shape[1], half), F32)
    return pl.pallas_call(
        weight_kernel,
        in_specs=[pl.BlockSpec(memory_space=pltpu.SMEM)] + [vmem] * 5,
        out_specs=[vmem] * 4,
        out_shape=[message] * 4,
        scratch_shapes=[pltpu.VMEM((half, half), F32)],
        compiler_params=pltpu.CompilerParams(vmem_limit_bytes=14 * 2**20),
        cost_estimate=pl.CostEstimate(
            flops=4 * mine.size * half, bytes_accessed=8 * mine.size, transcendentals=0
        ),
    )(lead, mine, others, own_grad, other_grad, lines)


def place_kernel(count, places_ref, *refs):
    pieces, out_ref, sems = refs[:count], refs[-2], refs[-1]
    copies = []
    for i, piece in enumerate(pieces):
        size = piece.shape[0]
        here = pl.ds(pl.multiple_of(places_ref[i], size), size)
        copies.append(pltpu.make_async_copy(piece, out_ref.at[here, :], sems.at[i]))
        copies[-1].start()
    for copy in copies:
        copy.wait()


def placed_rows(places, pieces, target):
    size, width = pieces[0].shape
    count = len(pieces)
    operands = list(pieces)
    specs = [pl.BlockSpec(memory_space=pltpu.VMEM)] * count
    if target is not None:
        operands += in_hbm([target])
        specs += [pl.BlockSpec(memory_space=pltpu.HBM)]
    return pl.pallas_call(
        functools.partial(place_kernel, count),
        in_specs=[pl.BlockSpec(memory_space=pltpu.SMEM)] + specs,
        out_specs=pl.BlockSpec(memory_space=pltpu.HBM),
        out_shape=pltpu.HBM((8 * size, width), F32),
        scratch_shapes=[pltpu.SemaphoreType.DMA((count,))],
        input_output_aliases={} if target is None else {count + 1: 0},
        compiler_params=pltpu.CompilerParams(vmem_limit_bytes=10 * 2**20),
    )(jnp.stack(places).astype(jnp.int32), *operands)


def solution(mesh):
    fine = Mesh(mesh.devices.reshape(4, 4, 2, 2, 2), ("x", "y", "c", "m", "t"))
    dp = ("x", "y", "c")
    placed = (P("t", dp, None), P("t", None, "m"), P(), P())
    return jax.shard_map(
        on_device,
        mesh=fine,
        in_specs=placed,
        out_specs=(P("t", dp + ("m",)), P("t", None, "m")),
        check_vma=False,
    )
```
